32 devices in a mesh: lon: 8 (over y, x, core), lat: 4 (over z).
Axes of the slice: x: 2, y: 2, z: 4, core: 2. Of those that a mesh axis runs over, the one named last changes fastest.
Arguments:
- send_species: float32 [1024, 16, 1024], P(('lon', 'lat')), may hold values from 0.1 to 4
- send_cells: int32 [1024, 1024], P(('lon', 'lat')), may hold values from 0 to 4095
- send_counts: int32 [1024], P(('lon', 'lat')), may hold values from 0 to 1024, as said below
- grid_state: float32 [16, 8, 32, 512], P(None, None, 'lon', 'lat'), may hold values from 0.1 to 4
- diff_rate: float32 [16], replicated, may hold values from 0.04 to 0.16
- prod_rate: float32 [16, 16], replicated, may hold values from 0 to 0.3
- loss_rate: float32 [16], replicated, may hold values from 0.05 to 20
- self_rate: float32 [16], replicated, may hold values from 0.05 to 2
Outputs:
- parcels_new: float32 [1024, 16, 1024], P(('lon', 'lat'))
- grid_mixed: float32 [16, 8, 32, 512], P(None, None, 'lon', 'lat')
The draws below stay inside these ranges and needn't reach their ends.
Inputs may be any that keep to these rules, and one draw needn't show every extreme that they name: `send_counts`: each source tile sends at most 1024 parcels to each tile. In every draw one tile receives exactly 1024 from every source, and at least a quarter of the tiles receive exactly 1024 from at least one source.
All inputs are finite; a program needn't handle non-finite values.
Results may differ from the reference program's by a relative error of at most 0.0011.
Values sent between devices are 32-bit elements; how exact they have to be, the bound alone decides.
A program may use at most 64 MiB of HBM per device.

```python
import math
import jax
import jax.numpy as jnp
from jax import lax

SPECIES = 16
LEVELS = 8
LON_DEV = 4
LAT_DEV = 128
ITERS = 4
SUBSTEPS = 2
DEVS = 32
CAP = 1024
CELLS_DEV = 4096
NLON = 32
NLAT = 512
N_LON = 8
N_LAT = 4


def draw_send_counts(key, part):
    key = jax.random.fold_in(key, 11)
    devices = N_LON * N_LAT
    key_list = jax.random.split(key, 4)
    light_load = jax.random.randint(key_list[0], (devices, devices), 7 * CAP // 8, CAP + 1)
    heavy_load = jax.random.randint(key_list[1], (devices, devices), 15 * CAP // 16, CAP + 1)
    ranking = jax.random.permutation(key_list[2], devices)
    chosen = jax.random.permutation(key_list[3], devices)
    source = jnp.arange(devices, dtype=jnp.int32)[:, None]
    busy_tile = (ranking < devices // 4)[None, :]
    counts = jnp.where(busy_tile, heavy_load, light_load)
    counts = jnp.where(busy_tile & (source == chosen[None, :]), CAP, counts)
    counts = jnp.where((ranking == 0)[None, :], CAP, counts)
    return counts.reshape(devices * devices).astype(jnp.int32)


def with_ends(result, rng, low, largest):
    longest = result.shape.index(max(result.shape))
    spots = []
    for shift in (0, 1):
        where = [jax.random.randint(jax.random.fold_in(rng, axis), (), 0, length) for axis, length in enumerate(result.shape)]
        where[longest] = (where[longest] + shift) % result.shape[longest]
        spots.append(tuple(where))
    return result.at[spots[0]].set(low).at[spots[1]].set(largest)


def block_levels(own_key, extent, cuts, low, top_value):
    level, own = 1.0, jax.random.fold_in(own_key, 6)
    for position, blocks in cuts:
        steps = jnp.exp(jax.random.uniform(jax.random.fold_in(own, position), (blocks,), jnp.float32, low / len(cuts), top_value / len(cuts)))
        level = level * jnp.repeat(steps, extent[position] // blocks).reshape([-1 if axis == position else 1 for axis in range(len(extent))])
    return level


def setup_inputs(seed: int = 0) -> dict:
    keys = jax.random.split(jax.random.key(seed), 9)
    return {
        "send_species": jnp.clip(jnp.exp(math.log(4.0) - 3.6888794 * jax.random.uniform(keys[0], (DEVS * DEVS, SPECIES, CAP), jnp.float32) ** block_levels(keys[0], (DEVS * DEVS, SPECIES, CAP), ((0, 32),), -0.2, 0.2)), 0.1, 4.0),
        "send_cells": with_ends(jax.random.randint(keys[1], (DEVS * DEVS, CAP), 0, CELLS_DEV), jax.random.fold_in(keys[1], 1), 0, CELLS_DEV - 1).astype(jnp.int32),
        "send_counts": draw_send_counts(jax.random.fold_in(keys[8], 71), 0),
        "grid_state": jnp.clip(jnp.exp(math.log(4.0) - 3.6888794 * jax.random.uniform(keys[3], (SPECIES, LEVELS, NLON, NLAT), jnp.float32) ** block_levels(keys[3], (SPECIES, LEVELS, NLON, NLAT), ((2, 8), (3, 4)), -0.2, 0.2)), 0.1, 4.0),
        "diff_rate": jnp.clip(jax.random.uniform(keys[4], (SPECIES,), jnp.float32, 0.04, 0.16), 0.04, 0.16),
        "prod_rate": jnp.clip(jax.random.uniform(keys[5], (SPECIES, SPECIES), jnp.float32, 0.0, 0.3), 0.0, 0.3),
        "loss_rate": jnp.clip(jnp.exp(jax.random.uniform(keys[6], (SPECIES,), jnp.float32, math.log(0.05), math.log(20.0))), 0.05, 20.0),
        "self_rate": jnp.clip(jnp.exp(jax.random.uniform(keys[7], (SPECIES,), jnp.float32, math.log(0.05), math.log(2.0))), 0.05, 2.0),
    }


grid_weight = 0.5
parcel_pull = 0.3


def diffuse(field_now, diff_rate):
    coefficient = diff_rate[:, None, None, None]
    for substep in range(SUBSTEPS):
        eastern = jnp.roll(field_now, -1, axis=2)
        western = jnp.roll(field_now, 1, axis=2)
        northern = jnp.concatenate([field_now[:, :, :, 1:], field_now[:, :, :, -1:]], axis=3)
        southern = jnp.concatenate([field_now[:, :, :, :1], field_now[:, :, :, :-1]], axis=3)
        above_cells = jnp.concatenate([field_now[:, 1:], field_now[:, -1:]], axis=1)
        below_cells = jnp.concatenate([field_now[:, :1], field_now[:, :-1]], axis=1)
        laplace = eastern + western + northern + southern + above_cells + below_cells - 6.0 * field_now
        field_now = field_now + coefficient * laplace
    return field_now


def reference(send_species, send_cells, send_counts, grid_state, diff_rate, prod_rate, loss_rate, self_rate):
    device_count = N_LON * N_LAT
    capacity = send_species.shape[2]
    cells_dev = LEVELS * LON_DEV * LAT_DEV
    diffused = diffuse(grid_state, diff_rate)
    tiles = diffused.reshape(SPECIES, LEVELS, N_LON, LON_DEV, N_LAT, LAT_DEV).transpose(2, 4, 0, 1, 3, 5).reshape(device_count, SPECIES, cells_dev)
    species = send_species.reshape(device_count, device_count, SPECIES, capacity).transpose(1, 0, 2, 3)
    cell_ids = send_cells.reshape(device_count, device_count, capacity).transpose(1, 0, 2)
    counts = send_counts.reshape(device_count, device_count).transpose(1, 0)

    def one_tile(tile_inputs):
        tile_grid, tile_species, tile_cells, tile_counts = tile_inputs
        alive_mask = jnp.arange(capacity, dtype=jnp.int32)[None, :] < tile_counts[:, None]
        live_weight = alive_mask.astype(jnp.float32)
        rounded = lax.optimization_barrier(tile_species.astype(jnp.bfloat16)).astype(jnp.float32)
        weighted = rounded * live_weight[:, None, :]
        flat_cells = tile_cells.reshape(-1)
        flat_species = weighted.transpose(1, 0, 2).reshape(SPECIES, -1)
        deposit = jnp.zeros((SPECIES, cells_dev), jnp.float32).at[:, flat_cells].add(flat_species)
        number = jnp.zeros((cells_dev,), jnp.float32).at[flat_cells].add(live_weight.reshape(-1))
        mixed_grid = (tile_grid + grid_weight * deposit) / (1.0 + grid_weight * number[None, :])
        coarse = lax.optimization_barrier(mixed_grid.astype(jnp.bfloat16)).astype(jnp.float32)
        at_parcel = coarse[:, flat_cells]
        initial = tile_species.transpose(1, 0, 2).reshape(SPECIES, -1)
        blended = initial + parcel_pull * (at_parcel - initial)
        concentration = blended
        for sweep in range(ITERS):
            produced = blended + jnp.dot(prod_rate, concentration, precision=lax.Precision.HIGHEST)
            concentration = produced / (1.0 + loss_rate[:, None] + self_rate[:, None] * concentration)
        reacted = concentration * live_weight.reshape(1, -1)
        return mixed_grid, reacted.reshape(SPECIES, device_count, capacity).transpose(1, 0, 2)

    grids, parcels = lax.map(one_tile, (tiles, species, cell_ids, counts))
    grid_mixed = grids.reshape(N_LON, N_LAT, SPECIES, LEVELS, LON_DEV, LAT_DEV).transpose(2, 3, 0, 4, 1, 5).reshape(SPECIES, LEVELS, NLON, NLAT)
    return parcels.reshape(device_count * device_count, SPECIES, capacity), grid_mixed
```

```python
import functools

import jax
import jax.numpy as jnp
from jax import lax
from jax.experimental import pallas as pl
from jax.experimental.pallas import tpu as pltpu
from jax.sharding import PartitionSpec as P

ITERS = 4
LOW = 256
WINDOW = 8

grid_weight = 0.5
parcel_pull = 0.3

f32 = jnp.float32
bf16 = jnp.bfloat16
MESH = pl.DeviceIdType.MESH


def hot_rows(index_row, count):
    wide = jnp.broadcast_to(index_row.astype(f32), (16, index_row.shape[1])).astype(bf16)
    rows = lax.broadcasted_iota(jnp.int32, (16, index_row.shape[1]), 0).astype(f32).astype(bf16)
    one = jnp.ones_like(wide)
    zero = jnp.zeros_like(wide)
    return jnp.concatenate(
        [jnp.where(wide == rows + float(16 * g), one, zero) for g in range(count // 16)], axis=0
    )


def exchange_kernel(
    n_lon,
    n_lat,
    species_hbm,
    cells_ref,
    counts_ref,
    grid_ref,
    rate_ref,
    prod_ref,
    loss_ref,
    self_ref,
    arrived_out,
    cells_out,
    diffused_out,
    deposit_out,
    weight_hi_out,
    weight_lo_out,
    rates_out,
    arrived,
    marked,
    cells_in,
    field,
    east_halo,
    west_halo,
    north_halo,
    south_halo,
    edges,
    send_sem,
    recv_sem,
    send_cell_sem,
    recv_cell_sem,
    out_sem,
    out_cell_sem,
    halo_send,
    halo_recv,
):
    devices = n_lon * n_lat
    species_count = 16
    capacity = cells_ref.shape[1]
    lon = lax.axis_index("lon")
    lat = lax.axis_index("lat")
    me = lon * n_lat + lat

    def partner(step, sign):
        a = step // n_lat
        b = lax.rem(step, n_lat)
        to_lon = lax.rem(lon + sign * a + n_lon, n_lon)
        to_lat = lax.rem(lat + sign * b + n_lat, n_lat)
        return to_lon, to_lat, to_lon * n_lat + to_lat

    barrier = pltpu.get_barrier_semaphore()

    def greet(step, carry):
        to_lon, to_lat, _ = partner(step, 1)
        pl.semaphore_signal(barrier, inc=1, device_id=(to_lon, to_lat), device_id_type=MESH)
        return carry

    lax.fori_loop(1, devices, greet, 0)

    own = pltpu.make_async_copy(species_hbm.at[me], arrived.at[me], recv_sem.at[me])
    own.start()

    slot = lax.broadcasted_iota(jnp.int32, (1, capacity), 1)

    def mark(row, carry):
        marked[row] = jnp.where(slot < counts_ref[row], cells_ref[pl.ds(row, 1), :], -1)
        return carry

    lax.fori_loop(0, devices, mark, 0)
    pl.semaphore_wait(barrier, devices - 1)

    def species_copy(to_lon, to_lat, tile):
        return pltpu.make_async_remote_copy(
            src_ref=species_hbm.at[tile],
            dst_ref=arrived.at[me],
            send_sem=send_sem.at[tile],
            recv_sem=recv_sem.at[me],
            device_id=(to_lon, to_lat),
            device_id_type=MESH,
        )

    def cells_copy(to_lon, to_lat, tile):
        return pltpu.make_async_remote_copy(
            src_ref=marked.at[tile],
            dst_ref=cells_in.at[me],
            send_sem=send_cell_sem.at[tile],
            recv_sem=recv_cell_sem.at[me],
            device_id=(to_lon, to_lat),
            device_id_type=MESH,
        )

    def send(step):
        to_lon, to_lat, tile = partner(step, 1)
        cells_copy(to_lon, to_lat, tile).start()
        species_copy(to_lon, to_lat, tile).start()

    def send_step(step, carry):
        send(step)
        return carry

    for j in range(4):
        for level in range(8):
            field[0, j, level] = grid_ref[:, level, j, :]

    def halo_copies(turn):
        up_lon = lax.rem(lon + 1, n_lon)
        down_lon = lax.rem(lon + n_lon - 1, n_lon)
        up_lat = lax.rem(lat + 1, n_lat)
        down_lat = lax.rem(lat + n_lat - 1, n_lat)
        plan = (
            (field.at[turn, 0], east_halo.at[turn], (down_lon, lat)),
            (field.at[turn, 3], west_halo.at[turn], (up_lon, lat)),
            (edges.at[turn, 0], north_halo.at[turn], (lon, down_lat)),
            (edges.at[turn, 1], south_halo.at[turn], (lon, up_lat)),
        )
        return [
            pltpu.make_async_remote_copy(
                src_ref=source,
                dst_ref=target,
                send_sem=halo_send.at[turn, k],
                recv_sem=halo_recv.at[turn, k],
                device_id=device,
                device_id_type=MESH,
            )
            for k, (source, target, device) in enumerate(plan)
        ]

    def halo_start(turn):
        edges[turn] = jnp.zeros_like(edges[turn])
        for j in range(4):
            turned = field[turn, j].reshape(128, 128).T
            edges[turn, 0, j : j + 1, :] = turned[0:1, :]
            edges[turn, 1, j : j + 1, :] = turned[127:128, :]
        for copy in halo_copies(turn):
            copy.start()

    def column(row, lane_count):
        pick = lax.broadcasted_iota(jnp.int32, (16, 16), 0) == lax.broadcasted_iota(
            jnp.int32, (16, 16), 1
        )
        return jnp.broadcast_to(
            jnp.sum(jnp.where(pick, row, 0.0), axis=1, keepdims=True), (16, lane_count)
        )

    rate = column(rate_ref[...], 128)
    lane = lax.broadcasted_iota(jnp.int32, (128, 128), 1)

    def diffuse(turn, store):
        for copy in halo_copies(turn):
            copy.wait()
        north_cols = north_halo[turn].T
        south_cols = south_halo[turn].T
        for j in range(4):
            v = field[turn, j].reshape(128, 128)
            east = east_halo[turn] if j == 3 else field[turn, j + 1]
            west = west_halo[turn] if j == 0 else field[turn, j - 1]
            north_col = jnp.broadcast_to(north_cols[:, j : j + 1], (128, 128))
            south_col = jnp.broadcast_to(south_cols[:, j : j + 1], (128, 128))
            north_edge = jnp.where(lat == n_lat - 1, v, north_col)
            south_edge = jnp.where(lat == 0, v, south_col)
            north = jnp.where(lane == 127, north_edge, pltpu.roll(v, 127, 1))
            south = jnp.where(lane == 0, south_edge, pltpu.roll(v, 1, 1))
            above = jnp.concatenate([v[16:], v[112:]], axis=0)
            below = jnp.concatenate([v[:16], v[:112]], axis=0)
            laplace = (
                east.reshape(128, 128)
                + west.reshape(128, 128)
                + north
                + south
                + above
                + below
                - 6.0 * v
            )
            store(j, (v + jnp.concatenate([rate] * 8, axis=0) * laplace).reshape(8, 16, 128))

    def store_field(j, value):
        field[1, j] = value

    def store_out(j, value):
        diffused_out[j] = value

    def deposit(tile):
        cells = cells_in[tile]
        rounded = arrived[tile].astype(bf16)
        low_hot = hot_rows(lax.bitwise_and(cells, LOW - 1), LOW)
        high = jnp.broadcast_to(lax.shift_right_arithmetic(cells, 8).astype(f32), (16, capacity))
        high = high.astype(bf16)
        zero = jnp.zeros_like(rounded)
        rows = lax.broadcasted_iota(jnp.int32, (16, capacity), 0).astype(f32).astype(bf16)
        spread = jnp.concatenate(
            [jnp.where(high == float(h), rounded, zero) for h in range(16)]
            + [jnp.where(high == rows, jnp.ones_like(zero), zero)],
            axis=0,
        )
        deposit_out[...] += lax.dot_general(
            spread, low_hot, (((1,), (1,)), ((), ())), preferred_element_type=f32
        )

    def keep(tile):
        pltpu.make_async_copy(arrived.at[tile], arrived_out.at[tile], out_sem.at[tile]).start()
        pltpu.make_async_copy(cells_in.at[tile], cells_out.at[tile], out_cell_sem.at[tile]).start()

    def receive(step, carry):
        from_lon, from_lat, tile = partner(step, -1)
        pltpu.make_async_remote_copy(
            src_ref=marked.at[tile],
            dst_ref=cells_in.at[tile],
            send_sem=send_cell_sem.at[tile],
            recv_sem=recv_cell_sem.at[tile],
            device_id=(from_lon, from_lat),
            device_id_type=MESH,
        ).wait_recv()
        pltpu.make_async_remote_copy(
            src_ref=species_hbm.at[tile],
            dst_ref=arrived.at[tile],
            send_sem=send_sem.at[tile],
            recv_sem=recv_sem.at[tile],
            device_id=(from_lon, from_lat),
            device_id_type=MESH,
        ).wait_recv()
        keep(tile)
        deposit(tile)
        return carry

    def receive_send(step, carry):
        receive(step, carry)
        send(step + WINDOW)
        return carry

    halo_start(0)
    lax.fori_loop(1, WINDOW + 1, send_step, 0)

    spot = lax.broadcasted_iota(jnp.int32, (256, 16), 0)
    spots = lax.broadcasted_iota(jnp.int32, (256, 16), 1)
    tall = jnp.where(lax.rem(spot, 16) == spots, 1.0, 0.0).astype(bf16)
    prod = prod_ref[...]
    prod_hi = prod.astype(bf16)
    prod_lo = (prod - prod_hi.astype(f32)).astype(bf16)
    row_group = lax.broadcasted_iota(jnp.int32, (256, 256), 0) // 16
    col_group = lax.broadcasted_iota(jnp.int32, (256, 256), 1) // 16
    for part, target in ((prod_hi, weight_hi_out), (prod_lo, weight_lo_out)):
        half = jnp.dot(tall, part, preferred_element_type=f32).astype(bf16)
        full = lax.dot_general(half, tall, (((1,), (1,)), ((), ())), preferred_element_type=f32)
        target[...] = jnp.where(row_group == col_group, full, 0.0).astype(bf16)
    rates_out[0] = jnp.concatenate([column(loss_ref[...], 128)] * 16, axis=0)
    rates_out[1] = jnp.concatenate([column(self_ref[...], 128)] * 16, axis=0)

    deposit_out[...] = jnp.zeros_like(deposit_out)
    cells_in[me] = marked[me]
    own.wait()
    keep(me)
    deposit(me)

    first = devices // 4
    second = devices // 2
    lax.fori_loop(1, first, receive_send, 0)
    diffuse(0, store_field)
    halo_start(1)
    lax.fori_loop(first, second, receive_send, 0)
    diffuse(1, store_out)
    lax.fori_loop(second, devices - WINDOW, receive_send, 0)
    lax.fori_loop(devices - WINDOW, devices, receive, 0)

    def finish(step, carry):
        to_lon, to_lat, tile = partner(step, 1)
        cells_copy(to_lon, to_lat, tile).wait_send()
        species_copy(to_lon, to_lat, tile).wait_send()
        return carry

    lax.fori_loop(1, devices, finish, 0)

    def finish_keep(tile, carry):
        pltpu.make_async_copy(arrived.at[tile], arrived_out.at[tile], out_sem.at[tile]).wait()
        pltpu.make_async_copy(cells_in.at[tile], cells_out.at[tile], out_cell_sem.at[tile]).wait()
        return carry

    lax.fori_loop(0, devices, finish_keep, 0)


def react_kernel(
    arrived_ref,
    cells_ref,
    diffused_ref,
    deposit_ref,
    weight_hi_ref,
    weight_lo_ref,
    rates_ref,
    parcels_ref,
    mixed_ref,
    coarse,
):
    @pl.when((pl.program_id(0) == 0) & (pl.program_id(1) == 0))
    def mix():
        for h in range(16):
            for side in range(2):
                lanes = slice(128 * side, 128 * (side + 1))
                j = 2 * (h % 2) + side
                number = deposit_ref[256 + h : 257 + h, lanes]
                value = (
                    diffused_ref[j, h // 2]
                    + grid_weight * deposit_ref[16 * h : 16 * (h + 1), lanes]
                ) / (1.0 + grid_weight * number)
                mixed_ref[:, h // 2, j, :] = value
                coarse[16 * h : 16 * (h + 1), lanes] = value.astype(bf16)

    lanes = arrived_ref.shape[2]
    chunk = min(lanes, 256)
    grid_now = coarse[...]

    def react(turn, carry):
        where = pl.ds(pl.multiple_of(turn * chunk, chunk), chunk)
        parts = []
        for source in range(16):
            cells = cells_ref[source, :, where]
            low_hot = hot_rows(lax.bitwise_and(cells, LOW - 1), LOW)
            picked = jnp.dot(grid_now, low_hot, preferred_element_type=f32)
            high = jnp.broadcast_to(lax.shift_right_arithmetic(cells, 8), (16, chunk))
            at_parcel = picked[:16]
            for h in range(1, 16):
                at_parcel = jnp.where(high == h, picked[16 * h : 16 * (h + 1)], at_parcel)
            start = arrived_ref[source, :, where]
            parts.append(start + parcel_pull * (at_parcel - start))
        blended = jnp.concatenate(parts, axis=0)
        state = blended
        loss = jnp.concatenate([rates_ref[0]] * (chunk // 128), axis=1)
        self_loss = jnp.concatenate([rates_ref[1]] * (chunk // 128), axis=1)
        for sweep in range(ITERS):
            high_part = state.astype(bf16)
            low_part = (state - high_part.astype(f32)).astype(bf16)
            produced = (
                blended
                + jnp.dot(weight_hi_ref[...], high_part, preferred_element_type=f32)
                + jnp.dot(weight_hi_ref[...], low_part, preferred_element_type=f32)
                + jnp.dot(weight_lo_ref[...], high_part, preferred_element_type=f32)
            )
            state = produced / (1.0 + loss + self_loss * state)
        for source in range(16):
            alive = jnp.broadcast_to(cells_ref[source, :, where] >= 0, (16, chunk))
            parcels_ref[source, :, where] = jnp.where(
                alive, state[16 * source : 16 * (source + 1)], 0.0
            )
        return carry

    lax.fori_loop(0, lanes // chunk, react, 0)


def local(
    send_species, send_cells, send_counts, grid_state, diff_rate, prod_rate, loss_rate, self_rate
):
    n_lon = lax.axis_size("lon")
    n_lat = lax.axis_size("lat")
    devices, species_count, capacity = send_species.shape
    vmem = pl.BlockSpec(memory_space=pltpu.VMEM)
    hbm = pl.BlockSpec(memory_space=pl.ANY)
    arrived, cells, diffused, deposit, weight_hi, weight_lo, rates = pl.pallas_call(
        functools.partial(exchange_kernel, n_lon, n_lat),
        out_shape=(
            jax.ShapeDtypeStruct((devices, species_count, capacity), f32),
            jax.ShapeDtypeStruct((devices, 1, capacity), jnp.int32),
            jax.ShapeDtypeStruct((4, 8, 16, 128), f32),
            jax.ShapeDtypeStruct((272, LOW), f32),
            jax.ShapeDtypeStruct((256, 256), bf16),
            jax.ShapeDtypeStruct((256, 256), bf16),
            jax.ShapeDtypeStruct((2, 256, 128), f32),
        ),
        in_specs=[
            hbm,
            vmem,
            pl.BlockSpec(memory_space=pltpu.SMEM),
            vmem,
            vmem,
            vmem,
            vmem,
            vmem,
        ],
        out_specs=(hbm, hbm, vmem, vmem, vmem, vmem, vmem),
        scratch_shapes=[
            pltpu.VMEM((devices, species_count, capacity), f32),
            pltpu.VMEM((devices, 1, capacity), jnp.int32),
            pltpu.VMEM((devices, 1, capacity), jnp.int32),
            pltpu.VMEM((2, 4, 8, 16, 128), f32),
            pltpu.VMEM((2, 8, 16, 128), f32),
            pltpu.VMEM((2, 8, 16, 128), f32),
            pltpu.VMEM((2, 8, 128), f32),
            pltpu.VMEM((2, 8, 128), f32),
            pltpu.VMEM((2, 2, 8, 128), f32),
            pltpu.SemaphoreType.DMA((devices,)),
            pltpu.SemaphoreType.DMA((devices,)),
            pltpu.SemaphoreType.DMA((devices,)),
            pltpu.SemaphoreType.DMA((devices,)),
            pltpu.SemaphoreType.DMA((devices,)),
            pltpu.SemaphoreType.DMA((devices,)),
            pltpu.SemaphoreType.DMA((2, 4)),
            pltpu.SemaphoreType.DMA((2, 4)),
        ],
        compiler_params=pltpu.CompilerParams(
            collective_id=0, has_side_effects=True, vmem_limit_bytes=40 * 1024 * 1024
        ),
        name="exchange",
    )(
        send_species,
        send_cells,
        send_counts,
        grid_state,
        diff_rate.reshape(1, 16),
        prod_rate,
        loss_rate.reshape(1, 16),
        self_rate.reshape(1, 16),
    )

    lanes = min(capacity, 512)
    whole = lambda shape: pl.BlockSpec(shape, lambda g, k: (0,) * len(shape))
    return pl.pallas_call(
        react_kernel,
        grid=(devices // 16, capacity // lanes),
        out_shape=(
            jax.ShapeDtypeStruct(send_species.shape, f32),
            jax.ShapeDtypeStruct(grid_state.shape, f32),
        ),
        in_specs=[
            pl.BlockSpec((16, 16, lanes), lambda g, k: (g, 0, k)),
            pl.BlockSpec((16, 1, lanes), lambda g, k: (g, 0, k)),
            whole((4, 8, 16, 128)),
            whole((272, LOW)),
            whole((256, 256)),
            whole((256, 256)),
            whole((2, 256, 128)),
        ],
        out_specs=(
            pl.BlockSpec((16, 16, lanes), lambda g, k: (g, 0, k)),
            whole(grid_state.shape),
        ),
        scratch_shapes=[pltpu.VMEM((256, LOW), bf16)],
        compiler_params=pltpu.CompilerParams(vmem_limit_bytes=40 * 1024 * 1024),
        name="react",
    )(arrived, cells, diffused, deposit, weight_hi, weight_lo, rates)


def solution(mesh):
    placed = (
        P(("lon", "lat"), None, None),
        P(("lon", "lat"), None),
        P(("lon", "lat")),
        P(None, None, "lon", "lat"),
        P(),
        P(),
        P(),
        P(),
    )
    return jax.shard_map(
        local,
        mesh=mesh,
        in_specs=placed,
        out_specs=(P(("lon", "lat"), None, None), P(None, None, "lon", "lat")),
        check_vma=False,
    )
```

```python
import functools

import jax
import jax.numpy as jnp
from jax import lax
from jax.experimental import pallas as pl
from jax.experimental.pallas import tpu as pltpu
from jax.sharding import PartitionSpec as P

ITERS = 4
LOW = 256
WINDOW = 16

grid_weight = 0.5
parcel_pull = 0.3

f32 = jnp.float32
bf16 = jnp.bfloat16
MESH = pl.DeviceIdType.MESH


def hot_rows(index_row, count):
    wide = jnp.broadcast_to(index_row.astype(f32), (16, index_row.shape[1])).astype(bf16)
    rows = lax.broadcasted_iota(jnp.int32, (16, index_row.shape[1]), 0).astype(f32).astype(bf16)
    one = jnp.ones_like(wide)
    zero = jnp.zeros_like(wide)
    return jnp.concatenate(
        [jnp.where(wide == rows + float(16 * g), one, zero) for g in range(count // 16)], axis=0
    )


def exchange_kernel(
    n_lon,
    n_lat,
    species_hbm,
    cells_hbm,
    counts_hbm,
    grid_hbm,
    rate_hbm,
    prod_hbm,
    loss_hbm,
    self_hbm,
    arrived_out,
    cells_out,
    diffused_out,
    deposit_out,
    weight_out,
    rates_out,
    cells_ref,
    counts_ref,
    grid_ref,
    rate_ref,
    prod_ref,
    loss_ref,
    self_ref,
    load_sem,
    arrived,
    marked,
    cells_in,
    field,
    east_halo,
    west_halo,
    north_halo,
    south_halo,
    edges,
    send_sem,
    recv_sem,
    send_cell_sem,
    recv_cell_sem,
    out_sem,
    out_cell_sem,
    halo_send,
    halo_recv,
):
    devices = n_lon * n_lat
    species_count = 16
    capacity = cells_ref.shape[1]
    lon = lax.axis_index("lon")
    lat = lax.axis_index("lat")
    me = lon * n_lat + lat

    def partner(step, sign):
        a = step // n_lat
        b = lax.rem(step, n_lat)
        to_lon = lax.rem(lon + sign * a + n_lon, n_lon)
        to_lat = lax.rem(lat + sign * b + n_lat, n_lat)
        return to_lon, to_lat, to_lon * n_lat + to_lat

    loads = [
        pltpu.make_async_copy(source, target, load_sem.at[k])
        for k, (source, target) in enumerate(
            (
                (cells_hbm, cells_ref),
                (counts_hbm, counts_ref),
                (grid_hbm, grid_ref),
                (rate_hbm, rate_ref),
                (prod_hbm, prod_ref),
                (loss_hbm, loss_ref),
                (self_hbm, self_ref),
            )
        )
    ]
    for load in loads:
        load.start()
    barrier = pltpu.get_barrier_semaphore()

    def greet(step, carry):
        to_lon, to_lat, _ = partner(step, 1)
        pl.semaphore_signal(barrier, inc=1, device_id=(to_lon, to_lat), device_id_type=MESH)
        return carry

    lax.fori_loop(1, devices, greet, 0)

    own = pltpu.make_async_copy(species_hbm.at[me], arrived.at[me], recv_sem.at[me])
    own.start()

    loads[0].wait()
    loads[1].wait()
    slot = lax.broadcasted_iota(jnp.int32, (1, capacity), 1)

    def mark(row, carry):
        marked[row] = jnp.where(slot < counts_ref[row], cells_ref[pl.ds(row, 1), :], -1)
        return carry

    lax.fori_loop(0, devices, mark, 0)
    pl.semaphore_wait(barrier, devices - 1)

    def species_copy(to_lon, to_lat, tile):
        return pltpu.make_async_remote_copy(
            src_ref=species_hbm.at[tile],
            dst_ref=arrived.at[me],
            send_sem=send_sem.at[tile],
            recv_sem=recv_sem.at[me],
            device_id=(to_lon, to_lat),
            device_id_type=MESH,
        )

    def cells_copy(to_lon, to_lat, tile):
        return pltpu.make_async_remote_copy(
            src_ref=marked.at[tile],
            dst_ref=cells_in.at[me],
            send_sem=send_cell_sem.at[tile],
            recv_sem=recv_cell_sem.at[me],
            device_id=(to_lon, to_lat),
            device_id_type=MESH,
        )

    def send(step):
        to_lon, to_lat, tile = partner(step, 1)
        cells_copy(to_lon, to_lat, tile).start()
        species_copy(to_lon, to_lat, tile).start()

    def send_step(step, carry):
        send(step)
        return carry

    lax.fori_loop(1, WINDOW + 1, send_step, 0)
    for load in loads[2:]:
        load.wait()

    for j in range(4):
        for level in range(8):
            field[0, j, level] = grid_ref[:, level, j, :]

    def halo_copies(turn):
        up_lon = lax.rem(lon + 1, n_lon)
        down_lon = lax.rem(lon + n_lon - 1, n_lon)
        up_lat = lax.rem(lat + 1, n_lat)
        down_lat = lax.rem(lat + n_lat - 1, n_lat)
        plan = (
            (field.at[turn, 0], east_halo.at[turn], (down_lon, lat)),
            (field.at[turn, 3], west_halo.at[turn], (up_lon, lat)),
            (edges.at[turn, 0], north_halo.at[turn], (lon, down_lat)),
            (edges.at[turn, 1], south_halo.at[turn], (lon, up_lat)),
        )
        return [
            pltpu.make_async_remote_copy(
                src_ref=source,
                dst_ref=target,
                send_sem=halo_send.at[turn, k],
                recv_sem=halo_recv.at[turn, k],
                device_id=device,
                device_id_type=MESH,
            )
            for k, (source, target, device) in enumerate(plan)
        ]

    def halo_start(turn):
        edges[turn] = jnp.zeros_like(edges[turn])
        for j in range(4):
            turned = field[turn, j].reshape(128, 128).T
            edges[turn, 0, j : j + 1, :] = turned[0:1, :]
            edges[turn, 1, j : j + 1, :] = turned[127:128, :]
        for copy in halo_copies(turn):
            copy.start()

    def column(row, lane_count):
        pick = lax.broadcasted_iota(jnp.int32, (16, 16), 0) == lax.broadcasted_iota(
            jnp.int32, (16, 16), 1
        )
        return jnp.broadcast_to(
            jnp.sum(jnp.where(pick, row, 0.0), axis=1, keepdims=True), (16, lane_count)
        )

    rate = column(rate_ref[...], 128)
    lane = lax.broadcasted_iota(jnp.int32, (128, 128), 1)

    def diffuse(turn, store):
        for copy in halo_copies(turn):
            copy.wait()
        north_cols = north_halo[turn].T
        south_cols = south_halo[turn].T
        for j in range(4):
            v = field[turn, j].reshape(128, 128)
            east = east_halo[turn] if j == 3 else field[turn, j + 1]
            west = west_halo[turn] if j == 0 else field[turn, j - 1]
            north_col = jnp.broadcast_to(north_cols[:, j : j + 1], (128, 128))
            south_col = jnp.broadcast_to(south_cols[:, j : j + 1], (128, 128))
            north_edge = jnp.where(lat == n_lat - 1, v, north_col)
            south_edge = jnp.where(lat == 0, v, south_col)
            north = jnp.where(lane == 127, north_edge, pltpu.roll(v, 127, 1))
            south = jnp.where(lane == 0, south_edge, pltpu.roll(v, 1, 1))
            above = jnp.concatenate([v[16:], v[112:]], axis=0)
            below = jnp.concatenate([v[:16], v[:112]], axis=0)
            laplace = (
                east.reshape(128, 128)
                + west.reshape(128, 128)
                + north
                + south
                + above
                + below
                - 6.0 * v
            )
            store(j, (v + jnp.concatenate([rate] * 8, axis=0) * laplace).reshape(8, 16, 128))

    def store_field(j, value):
        field[1, j] = value

    def store_out(j, value):
        diffused_out[j] = value

    def deposit(tile):
        cells = cells_in[tile]
        rounded = arrived[tile].astype(bf16)
        low_hot = hot_rows(lax.bitwise_and(cells, LOW - 1), LOW)
        high = jnp.broadcast_to(lax.shift_right_arithmetic(cells, 8).astype(f32), (16, capacity))
        high = high.astype(bf16)
        zero = jnp.zeros_like(rounded)
        rows = lax.broadcasted_iota(jnp.int32, (16, capacity), 0).astype(f32).astype(bf16)
        spread = jnp.concatenate(
            [jnp.where(high == float(h), rounded, zero) for h in range(16)]
            + [jnp.where(high == rows, jnp.ones_like(zero), zero)],
            axis=0,
        )
        deposit_out[...] += lax.dot_general(
            spread, low_hot, (((1,), (1,)), ((), ())), preferred_element_type=f32
        )

    def keep(tile):
        pltpu.make_async_copy(arrived.at[tile], arrived_out.at[tile], out_sem.at[tile]).start()
        pltpu.make_async_copy(cells_in.at[tile], cells_out.at[tile], out_cell_sem.at[tile]).start()

    def receive(step, carry):
        from_lon, from_lat, tile = partner(step, -1)
        pltpu.make_async_remote_copy(
            src_ref=marked.at[tile],
            dst_ref=cells_in.at[tile],
            send_sem=send_cell_sem.at[tile],
            recv_sem=recv_cell_sem.at[tile],
            device_id=(from_lon, from_lat),
            device_id_type=MESH,
        ).wait_recv()
        pltpu.make_async_remote_copy(
            src_ref=species_hbm.at[tile],
            dst_ref=arrived.at[tile],
            send_sem=send_sem.at[tile],
            recv_sem=recv_sem.at[tile],
            device_id=(from_lon, from_lat),
            device_id_type=MESH,
        ).wait_recv()
        keep(tile)
        deposit(tile)
        return carry

    def receive_send(step, carry):
        receive(step, carry)
        send(step + WINDOW)
        return carry

    halo_start(0)

    spot = lax.broadcasted_iota(jnp.int32, (256, 16), 0)
    spots = lax.broadcasted_iota(jnp.int32, (256, 16), 1)
    tall = jnp.where(lax.rem(spot, 16) == spots, 1.0, 0.0).astype(bf16)
    prod = prod_ref[...]
    prod_hi = prod.astype(bf16)
    prod_lo = (prod - prod_hi.astype(f32)).astype(bf16)
    row = lax.broadcasted_iota(jnp.int32, (256, 256), 0)
    col = lax.broadcasted_iota(jnp.int32, (256, 256), 1)
    same = lax.rem(row // 16, 8) == lax.rem(col // 16, 8)
    wide = []
    for part in (prod_hi, prod_lo):
        half = jnp.dot(tall, part, preferred_element_type=f32).astype(bf16)
        wide.append(
            lax.dot_general(half, tall, (((1,), (1,)), ((), ())), preferred_element_type=f32)
        )
    weight_out[...] = jnp.where(
        same, jnp.where(row < 128, wide[0], jnp.where(col < 128, wide[1], 0.0)), 0.0
    ).astype(bf16)
    rates_out[0] = jnp.concatenate([1.0 + column(loss_ref[...], 128)] * 8, axis=0)
    rates_out[1] = jnp.concatenate([column(self_ref[...], 128)] * 8, axis=0)

    deposit_out[...] = jnp.zeros_like(deposit_out)
    cells_in[me] = marked[me]
    own.wait()
    keep(me)
    deposit(me)

    first = devices // 4
    second = devices // 2
    lax.fori_loop(1, first, receive_send, 0)
    diffuse(0, store_field)
    halo_start(1)
    lax.fori_loop(first, second, receive_send, 0)
    diffuse(1, store_out)
    lax.fori_loop(second, devices - WINDOW, receive_send, 0)
    lax.fori_loop(devices - WINDOW, devices, receive, 0)

    def finish(step, carry):
        to_lon, to_lat, tile = partner(step, 1)
        cells_copy(to_lon, to_lat, tile).wait_send()
        species_copy(to_lon, to_lat, tile).wait_send()
        return carry

    lax.fori_loop(1, devices, finish, 0)

    def finish_keep(tile, carry):
        pltpu.make_async_copy(arrived.at[tile], arrived_out.at[tile], out_sem.at[tile]).wait()
        pltpu.make_async_copy(cells_in.at[tile], cells_out.at[tile], out_cell_sem.at[tile]).wait()
        return carry

    lax.fori_loop(0, devices, finish_keep, 0)


def react_kernel(
    arrived_ref,
    cells_ref,
    diffused_ref,
    deposit_ref,
    weight_ref,
    rates_ref,
    parcels_ref,
    mixed_ref,
    coarse,
):
    @pl.when((pl.program_id(0) == 0) & (pl.program_id(1) == 0))
    def mix():
        for h in range(16):
            for side in range(2):
                lanes = slice(128 * side, 128 * (side + 1))
                j = 2 * (h % 2) + side
                number = deposit_ref[256 + h : 257 + h, lanes]
                value = (
                    diffused_ref[j, h // 2]
                    + grid_weight * deposit_ref[16 * h : 16 * (h + 1), lanes]
                ) / (1.0 + grid_weight * number)
                mixed_ref[:, h // 2, j, :] = value
                coarse[16 * h : 16 * (h + 1), lanes] = value.astype(bf16)

    lanes = arrived_ref.shape[2]
    chunk = min(lanes, 256)
    grid_now = coarse[...]
    loss = jnp.concatenate([rates_ref[0]] * (chunk // 128), axis=1)
    self_loss = jnp.concatenate([rates_ref[1]] * (chunk // 128), axis=1)

    def blend(source, where):
        cells = cells_ref[source, :, where]
        low_hot = hot_rows(lax.bitwise_and(cells, LOW - 1), LOW)
        picked = jnp.dot(grid_now, low_hot, preferred_element_type=f32)
        found = [picked[16 * h : 16 * (h + 1)] for h in range(16)]
        for bit in range(4):
            is_set = lax.bitwise_and(cells, LOW << bit) != 0
            is_set = jnp.broadcast_to(is_set, (16, chunk))
            found = [
                jnp.where(is_set, found[2 * k + 1], found[2 * k]) for k in range(len(found) // 2)
            ]
        start = arrived_ref[source, :, where]
        return start + parcel_pull * (found[0] - start)

    for turn in range(lanes // chunk):
        where = slice(chunk * turn, chunk * (turn + 1))
        for first in range(0, 16, 8):
            blended = jnp.concatenate(
                [blend(source, where) for source in range(first, first + 8)], axis=0
            )
            state = blended
            for sweep in range(ITERS):
                high_part = state.astype(bf16)
                low_part = (state - high_part.astype(f32)).astype(bf16)
                product = jnp.dot(
                    weight_ref[...],
                    jnp.concatenate([high_part, low_part], axis=0),
                    preferred_element_type=f32,
                )
                produced = blended + (product[:128] + product[128:])
                bottom = loss + self_loss * state
                inverse = pl.reciprocal(bottom, approx=True)
                state = produced * (inverse * (2.0 - bottom * inverse))
            for k in range(8):
                alive = jnp.broadcast_to(cells_ref[first + k, :, where] >= 0, (16, chunk))
                parcels_ref[first + k, :, where] = jnp.where(
                    alive, state[16 * k : 16 * (k + 1)], 0.0
                )


def local(
    send_species, send_cells, send_counts, grid_state, diff_rate, prod_rate, loss_rate, self_rate
):
    n_lon = lax.axis_size("lon")
    n_lat = lax.axis_size("lat")
    devices, species_count, capacity = send_species.shape
    vmem = pl.BlockSpec(memory_space=pltpu.VMEM)
    hbm = pl.BlockSpec(memory_space=pl.ANY)
    arrived, cells, diffused, deposit, weight, rates = pl.pallas_call(
        functools.partial(exchange_kernel, n_lon, n_lat),
        out_shape=(
            jax.ShapeDtypeStruct((devices, species_count, capacity), f32),
            jax.ShapeDtypeStruct((devices, 1, capacity), jnp.int32),
            jax.ShapeDtypeStruct((4, 8, 16, 128), f32),
            jax.ShapeDtypeStruct((272, LOW), f32),
            jax.ShapeDtypeStruct((256, 256), bf16),
            jax.ShapeDtypeStruct((2, 128, 128), f32),
        ),
        in_specs=[pl.BlockSpec(memory_space=pltpu.HBM)] * 8,
        out_specs=(hbm, hbm, vmem, vmem, vmem, vmem),
        scratch_shapes=[
            pltpu.VMEM(send_cells.shape, jnp.int32),
            pltpu.SMEM(send_counts.shape, jnp.int32),
            pltpu.VMEM(grid_state.shape, f32),
            pltpu.VMEM((1, 16), f32),
            pltpu.VMEM((16, 16), f32),
            pltpu.VMEM((1, 16), f32),
            pltpu.VMEM((1, 16), f32),
            pltpu.SemaphoreType.DMA((7,)),
            pltpu.VMEM((devices, species_count, capacity), f32),
            pltpu.VMEM((devices, 1, capacity), jnp.int32),
            pltpu.VMEM((devices, 1, capacity), jnp.int32),
            pltpu.VMEM((2, 4, 8, 16, 128), f32),
            pltpu.VMEM((2, 8, 16, 128), f32),
            pltpu.VMEM((2, 8, 16, 128), f32),
            pltpu.VMEM((2, 8, 128), f32),
            pltpu.VMEM((2, 8, 128), f32),
            pltpu.VMEM((2, 2, 8, 128), f32),
            pltpu.SemaphoreType.DMA((devices,)),
            pltpu.SemaphoreType.DMA((devices,)),
            pltpu.SemaphoreType.DMA((devices,)),
            pltpu.SemaphoreType.DMA((devices,)),
            pltpu.SemaphoreType.DMA((devices,)),
            pltpu.SemaphoreType.DMA((devices,)),
            pltpu.SemaphoreType.DMA((2, 4)),
            pltpu.SemaphoreType.DMA((2, 4)),
        ],
        compiler_params=pltpu.CompilerParams(
            collective_id=0, has_side_effects=True, vmem_limit_bytes=40 * 1024 * 1024
        ),
        name="exchange",
    )(
        send_species,
        send_cells,
        send_counts,
        grid_state,
        diff_rate.reshape(1, 16),
        prod_rate,
        loss_rate.reshape(1, 16),
        self_rate.reshape(1, 16),
    )

    lanes = min(capacity, 512)
    whole = lambda shape: pl.BlockSpec(shape, lambda g, k: (0,) * len(shape))
    return pl.pallas_call(
        react_kernel,
        grid=(devices // 16, capacity // lanes),
        out_shape=(
            jax.ShapeDtypeStruct(send_species.shape, f32),
            jax.ShapeDtypeStruct(grid_state.shape, f32),
        ),
        in_specs=[
            pl.BlockSpec((16, 16, lanes), lambda g, k: (g, 0, k)),
            pl.BlockSpec((16, 1, lanes), lambda g, k: (g, 0, k)),
            whole((4, 8, 16, 128)),
            whole((272, LOW)),
            whole((256, 256)),
            whole((2, 128, 128)),
        ],
        out_specs=(
            pl.BlockSpec((16, 16, lanes), lambda g, k: (g, 0, k)),
            whole(grid_state.shape),
        ),
        scratch_shapes=[pltpu.VMEM((256, LOW), bf16)],
        compiler_params=pltpu.CompilerParams(vmem_limit_bytes=40 * 1024 * 1024),
        name="react",
    )(arrived, cells, diffused, deposit, weight, rates)


def solution(mesh):
    placed = (
        P(("lon", "lat"), None, None),
        P(("lon", "lat"), None),
        P(("lon", "lat")),
        P(None, None, "lon", "lat"),
        P(),
        P(),
        P(),
        P(),
    )
    return jax.shard_map(
        local,
        mesh=mesh,
        in_specs=placed,
        out_specs=(P(("lon", "lat"), None, None), P(None, None, "lon", "lat")),
        check_vma=False,
    )
```

```python
import functools

import jax
import jax.numpy as jnp
from jax import lax
from jax.experimental import pallas as pl
from jax.experimental.pallas import tpu as pltpu
from jax.sharding import PartitionSpec as P

ITERS = 4
LOW = 256
WINDOW = 31
VMEM_BYTES = 62 * 1024 * 1024

grid_weight = 0.5
parcel_pull = 0.3

f32 = jnp.float32
bf16 = jnp.bfloat16
MESH = pl.DeviceIdType.MESH


def hot_rows(index_row, count):
    wide = jnp.broadcast_to(index_row.astype(f32), (16, index_row.shape[1])).astype(bf16)
    rows = lax.broadcasted_iota(jnp.int32, (16, index_row.shape[1]), 0).astype(f32).astype(bf16)
    one = jnp.ones_like(wide)
    zero = jnp.zeros_like(wide)
    return jnp.concatenate(
        [jnp.where(wide == rows + float(16 * g), one, zero) for g in range(count // 16)], axis=0
    )


def exchange_kernel(
    n_lon,
    n_lat,
    species_hbm,
    cells_hbm,
    counts_hbm,
    grid_hbm,
    rate_hbm,
    prod_hbm,
    loss_hbm,
    self_hbm,
    arrived_out,
    cells_out,
    diffused_out,
    deposit_out,
    weight_out,
    rates_out,
    cells_ref,
    counts_ref,
    grid_ref,
    rate_ref,
    prod_ref,
    loss_ref,
    self_ref,
    load_sem,
    arrived,
    marked,
    cells_in,
    field,
    east_halo,
    west_halo,
    north_halo,
    south_halo,
    edges,
    send_sem,
    recv_sem,
    send_cell_sem,
    recv_cell_sem,
    out_sem,
    out_cell_sem,
    halo_send,
    halo_recv,
):
    devices = n_lon * n_lat
    species_count = 16
    capacity = cells_ref.shape[1]
    lon = lax.axis_index("lon")
    lat = lax.axis_index("lat")
    me = lon * n_lat + lat

    def partner(step, sign):
        a = step // n_lat
        b = lax.rem(step, n_lat)
        to_lon = lax.rem(lon + sign * a + n_lon, n_lon)
        to_lat = lax.rem(lat + sign * b + n_lat, n_lat)
        return to_lon, to_lat, to_lon * n_lat + to_lat

    loads = [
        pltpu.make_async_copy(source, target, load_sem.at[k])
        for k, (source, target) in enumerate(
            (
                (cells_hbm, cells_ref),
                (counts_hbm, counts_ref),
                (grid_hbm, grid_ref),
                (rate_hbm, rate_ref),
                (prod_hbm, prod_ref),
                (loss_hbm, loss_ref),
                (self_hbm, self_ref),
            )
        )
    ]
    for load in loads:
        load.start()
    barrier = pltpu.get_barrier_semaphore()

    def greet(step, carry):
        to_lon, to_lat, _ = partner(step, 1)
        pl.semaphore_signal(barrier, inc=1, device_id=(to_lon, to_lat), device_id_type=MESH)
        return carry

    lax.fori_loop(1, devices, greet, 0)

    own = pltpu.make_async_copy(species_hbm.at[me], arrived.at[me], recv_sem.at[me])
    own.start()

    loads[0].wait()
    loads[1].wait()
    slot = lax.broadcasted_iota(jnp.int32, (1, capacity), 1)

    def mark(row, carry):
        marked[row] = jnp.where(slot < counts_ref[row], cells_ref[pl.ds(row, 1), :], -1)
        return carry

    lax.fori_loop(0, devices, mark, 0)
    pl.semaphore_wait(barrier, devices - 1)

    def species_copy(to_lon, to_lat, tile):
        return pltpu.make_async_remote_copy(
            src_ref=species_hbm.at[tile],
            dst_ref=arrived.at[me],
            send_sem=send_sem.at[tile],
            recv_sem=recv_sem.at[me],
            device_id=(to_lon, to_lat),
            device_id_type=MESH,
        )

    def cells_copy(to_lon, to_lat, tile):
        return pltpu.make_async_remote_copy(
            src_ref=marked.at[tile],
            dst_ref=cells_in.at[me],
            send_sem=send_cell_sem.at[tile],
            recv_sem=recv_cell_sem.at[me],
            device_id=(to_lon, to_lat),
            device_id_type=MESH,
        )

    def send(step):
        to_lon, to_lat, tile = partner(step, 1)
        cells_copy(to_lon, to_lat, tile).start()
        species_copy(to_lon, to_lat, tile).start()

    def send_step(step, carry):
        send(step)
        return carry

    lax.fori_loop(1, WINDOW + 1, send_step, 0)
    for load in loads[2:]:
        load.wait()

    for j in range(4):
        for level in range(8):
            field[0, j, level] = grid_ref[:, level, j, :]

    def halo_copies(turn):
        up_lon = lax.rem(lon + 1, n_lon)
        down_lon = lax.rem(lon + n_lon - 1, n_lon)
        up_lat = lax.rem(lat + 1, n_lat)
        down_lat = lax.rem(lat + n_lat - 1, n_lat)
        plan = (
            (field.at[turn, 0], east_halo.at[turn], (down_lon, lat)),
            (field.at[turn, 3], west_halo.at[turn], (up_lon, lat)),
            (edges.at[turn, 0], north_halo.at[turn], (lon, down_lat)),
            (edges.at[turn, 1], south_halo.at[turn], (lon, up_lat)),
        )
        return [
            pltpu.make_async_remote_copy(
                src_ref=source,
                dst_ref=target,
                send_sem=halo_send.at[turn, k],
                recv_sem=halo_recv.at[turn, k],
                device_id=device,
                device_id_type=MESH,
            )
            for k, (source, target, device) in enumerate(plan)
        ]

    def halo_start(turn):
        edges[turn] = jnp.zeros_like(edges[turn])
        for j in range(4):
            turned = field[turn, j].reshape(128, 128).T
            edges[turn, 0, j : j + 1, :] = turned[0:1, :]
            edges[turn, 1, j : j + 1, :] = turned[127:128, :]
        for copy in halo_copies(turn):
            copy.start()

    def column(row, lane_count):
        pick = lax.broadcasted_iota(jnp.int32, (16, 16), 0) == lax.broadcasted_iota(
            jnp.int32, (16, 16), 1
        )
        return jnp.broadcast_to(
            jnp.sum(jnp.where(pick, row, 0.0), axis=1, keepdims=True), (16, lane_count)
        )

    rate = column(rate_ref[...], 128)
    lane = lax.broadcasted_iota(jnp.int32, (128, 128), 1)

    def diffuse(turn, store):
        for copy in halo_copies(turn):
            copy.wait()
        north_cols = north_halo[turn].T
        south_cols = south_halo[turn].T
        for j in range(4):
            v = field[turn, j].reshape(128, 128)
            east = east_halo[turn] if j == 3 else field[turn, j + 1]
            west = west_halo[turn] if j == 0 else field[turn, j - 1]
            north_col = jnp.broadcast_to(north_cols[:, j : j + 1], (128, 128))
            south_col = jnp.broadcast_to(south_cols[:, j : j + 1], (128, 128))
            north_edge = jnp.where(lat == n_lat - 1, v, north_col)
            south_edge = jnp.where(lat == 0, v, south_col)
            north = jnp.where(lane == 127, north_edge, pltpu.roll(v, 127, 1))
            south = jnp.where(lane == 0, south_edge, pltpu.roll(v, 1, 1))
            above = jnp.concatenate([v[16:], v[112:]], axis=0)
            below = jnp.concatenate([v[:16], v[:112]], axis=0)
            laplace = (
                east.reshape(128, 128)
                + west.reshape(128, 128)
                + north
                + south
                + above
                + below
                - 6.0 * v
            )
            store(j, (v + jnp.concatenate([rate] * 8, axis=0) * laplace).reshape(8, 16, 128))

    def store_field(j, value):
        field[1, j] = value

    def store_out(j, value):
        diffused_out[j] = value

    def deposit(tile):
        cells = cells_in[tile]
        rounded = arrived[tile].astype(bf16)
        low_hot = hot_rows(lax.bitwise_and(cells, LOW - 1), LOW)
        high = jnp.broadcast_to(lax.shift_right_arithmetic(cells, 8).astype(f32), (16, capacity))
        high = high.astype(bf16)
        zero = jnp.zeros_like(rounded)
        rows = lax.broadcasted_iota(jnp.int32, (16, capacity), 0).astype(f32).astype(bf16)
        spread = jnp.concatenate(
            [jnp.where(high == float(h), rounded, zero) for h in range(16)]
            + [jnp.where(high == rows, jnp.ones_like(zero), zero)],
            axis=0,
        )
        deposit_out[...] += lax.dot_general(
            spread, low_hot, (((1,), (1,)), ((), ())), preferred_element_type=f32
        )

    def keep(tile):
        pltpu.make_async_copy(arrived.at[tile], arrived_out.at[tile], out_sem.at[tile]).start()
        pltpu.make_async_copy(cells_in.at[tile], cells_out.at[tile], out_cell_sem.at[tile]).start()

    def receive(step, carry):
        from_lon, from_lat, tile = partner(step, -1)
        pltpu.make_async_remote_copy(
            src_ref=marked.at[tile],
            dst_ref=cells_in.at[tile],
            send_sem=send_cell_sem.at[tile],
            recv_sem=recv_cell_sem.at[tile],
            device_id=(from_lon, from_lat),
            device_id_type=MESH,
        ).wait_recv()
        pltpu.make_async_remote_copy(
            src_ref=species_hbm.at[tile],
            dst_ref=arrived.at[tile],
            send_sem=send_sem.at[tile],
            recv_sem=recv_sem.at[tile],
            device_id=(from_lon, from_lat),
            device_id_type=MESH,
        ).wait_recv()
        keep(tile)
        deposit(tile)
        return carry

    def receive_send(step, carry):
        receive(step, carry)

        @pl.when(step + WINDOW < devices)
        def refill():
            send(step + WINDOW)

        return carry

    halo_start(0)

    spot = lax.broadcasted_iota(jnp.int32, (256, 16), 0)
    spots = lax.broadcasted_iota(jnp.int32, (256, 16), 1)
    tall = jnp.where(lax.rem(spot, 16) == spots, 1.0, 0.0).astype(bf16)
    prod = prod_ref[...]
    prod_hi = prod.astype(bf16)
    prod_lo = (prod - prod_hi.astype(f32)).astype(bf16)
    row = lax.broadcasted_iota(jnp.int32, (256, 256), 0)
    col = lax.broadcasted_iota(jnp.int32, (256, 256), 1)
    same = lax.rem(row // 16, 8) == lax.rem(col // 16, 8)
    wide = []
    for part in (prod_hi, prod_lo):
        half = jnp.dot(tall, part, preferred_element_type=f32).astype(bf16)
        wide.append(
            lax.dot_general(half, tall, (((1,), (1,)), ((), ())), preferred_element_type=f32)
        )
    weight_out[...] = jnp.where(
        same, jnp.where(row < 128, wide[0], jnp.where(col < 128, wide[1], 0.0)), 0.0
    ).astype(bf16)
    rates_out[0] = jnp.concatenate([1.0 + column(loss_ref[...], 128)] * 8, axis=0)
    rates_out[1] = jnp.concatenate([column(self_ref[...], 128)] * 8, axis=0)

    deposit_out[...] = jnp.zeros_like(deposit_out)
    cells_in[me] = marked[me]
    own.wait()
    keep(me)
    deposit(me)

    first = devices // 4
    second = devices // 2
    lax.fori_loop(1, first, receive_send, 0)
    diffuse(0, store_field)
    halo_start(1)
    lax.fori_loop(first, second, receive_send, 0)
    diffuse(1, store_out)
    lax.fori_loop(second, devices, receive_send, 0)

    def finish(step, carry):
        to_lon, to_lat, tile = partner(step, 1)
        cells_copy(to_lon, to_lat, tile).wait_send()
        species_copy(to_lon, to_lat, tile).wait_send()
        return carry

    lax.fori_loop(1, devices, finish, 0)

    def finish_keep(tile, carry):
        pltpu.make_async_copy(arrived.at[tile], arrived_out.at[tile], out_sem.at[tile]).wait()
        pltpu.make_async_copy(cells_in.at[tile], cells_out.at[tile], out_cell_sem.at[tile]).wait()
        return carry

    lax.fori_loop(0, devices, finish_keep, 0)


def react_kernel(
    arrived_ref,
    cells_ref,
    diffused_ref,
    deposit_ref,
    weight_ref,
    rates_ref,
    parcels_ref,
    mixed_ref,
    coarse,
    blended,
):
    @pl.when((pl.program_id(0) == 0) & (pl.program_id(1) == 0))
    def mix():
        for h in range(16):
            for side in range(2):
                lanes = slice(128 * side, 128 * (side + 1))
                j = 2 * (h % 2) + side
                number = deposit_ref[256 + h : 257 + h, lanes]
                value = (
                    diffused_ref[j, h // 2]
                    + grid_weight * deposit_ref[16 * h : 16 * (h + 1), lanes]
                ) / (1.0 + grid_weight * number)
                mixed_ref[:, h // 2, j, :] = value
                coarse[16 * h : 16 * (h + 1), lanes] = value.astype(bf16)

    lanes = arrived_ref.shape[2]
    chunk = min(lanes, 256)
    chunks = [slice(k, k + chunk) for k in range(0, lanes, chunk)]
    loss = jnp.concatenate([rates_ref[0]] * (chunk // 128), axis=1)
    self_loss = jnp.concatenate([rates_ref[1]] * (chunk // 128), axis=1)

    def blend(source, carry):
        for where in chunks:
            cells = cells_ref[source, :, where]
            low_hot = hot_rows(lax.bitwise_and(cells, LOW - 1), LOW)
            picked = jnp.dot(coarse[...], low_hot, preferred_element_type=f32)
            high = jnp.broadcast_to(lax.shift_right_arithmetic(cells, 8), (16, chunk))
            found = picked[:16]
            for h in range(1, 16):
                found = jnp.where(high == h, picked[16 * h : 16 * (h + 1)], found)
            start = arrived_ref[source, :, where]
            blended[source, :, where] = start + parcel_pull * (found - start)
        return carry

    lax.fori_loop(0, 16, blend, 0, unroll=2)

    groups = [(first, where) for where in chunks for first in (0, 8)]
    starts = [
        blended[first : first + 8, :, where].reshape(128, chunk) for first, where in groups
    ]
    states = starts
    for sweep in range(ITERS):
        parts = []
        for state in states:
            high_part = state.astype(bf16)
            low_part = (state - high_part.astype(f32)).astype(bf16)
            parts.append(jnp.concatenate([high_part, low_part], axis=0))
        products = [jnp.dot(weight_ref[...], part, preferred_element_type=f32) for part in parts]
        later = []
        for start, state, product in zip(starts, states, products):
            produced = start + (product[:128] + product[128:])
            bottom = loss + self_loss * state
            inverse = pl.reciprocal(bottom, approx=True)
            later.append(produced * (inverse * (2.0 - bottom * inverse)))
        states = later
    for (first, where), state in zip(groups, states):
        for k in range(8):
            alive = jnp.broadcast_to(cells_ref[first + k, :, where] >= 0, (16, chunk))
            parcels_ref[first + k, :, where] = jnp.where(
                alive, state[16 * k : 16 * (k + 1)], 0.0
            )


def local(
    send_species, send_cells, send_counts, grid_state, diff_rate, prod_rate, loss_rate, self_rate
):
    n_lon = lax.axis_size("lon")
    n_lat = lax.axis_size("lat")
    devices, species_count, capacity = send_species.shape
    vmem = pl.BlockSpec(memory_space=pltpu.VMEM)
    hbm = pl.BlockSpec(memory_space=pl.ANY)
    arrived, cells, diffused, deposit, weight, rates = pl.pallas_call(
        functools.partial(exchange_kernel, n_lon, n_lat),
        out_shape=(
            jax.ShapeDtypeStruct((devices, species_count, capacity), f32),
            jax.ShapeDtypeStruct((devices, 1, capacity), jnp.int32),
            jax.ShapeDtypeStruct((4, 8, 16, 128), f32),
            jax.ShapeDtypeStruct((272, LOW), f32),
            jax.ShapeDtypeStruct((256, 256), bf16),
            jax.ShapeDtypeStruct((2, 128, 128), f32),
        ),
        in_specs=[pl.BlockSpec(memory_space=pltpu.HBM)] * 8,
        out_specs=(hbm, hbm, vmem, vmem, vmem, vmem),
        scratch_shapes=[
            pltpu.VMEM(send_cells.shape, jnp.int32),
            pltpu.SMEM(send_counts.shape, jnp.int32),
            pltpu.VMEM(grid_state.shape, f32),
            pltpu.VMEM((1, 16), f32),
            pltpu.VMEM((16, 16), f32),
            pltpu.VMEM((1, 16), f32),
            pltpu.VMEM((1, 16), f32),
            pltpu.SemaphoreType.DMA((7,)),
            pltpu.VMEM((devices, species_count, capacity), f32),
            pltpu.VMEM((devices, 1, capacity), jnp.int32),
            pltpu.VMEM((devices, 1, capacity), jnp.int32),
            pltpu.VMEM((2, 4, 8, 16, 128), f32),
            pltpu.VMEM((2, 8, 16, 128), f32),
            pltpu.VMEM((2, 8, 16, 128), f32),
            pltpu.VMEM((2, 8, 128), f32),
            pltpu.VMEM((2, 8, 128), f32),
            pltpu.VMEM((2, 2, 8, 128), f32),
            pltpu.SemaphoreType.DMA((devices,)),
            pltpu.SemaphoreType.DMA((devices,)),
            pltpu.SemaphoreType.DMA((devices,)),
            pltpu.SemaphoreType.DMA((devices,)),
            pltpu.SemaphoreType.DMA((devices,)),
            pltpu.SemaphoreType.DMA((devices,)),
            pltpu.SemaphoreType.DMA((2, 4)),
            pltpu.SemaphoreType.DMA((2, 4)),
        ],
        compiler_params=pltpu.CompilerParams(
            collective_id=0, has_side_effects=True, vmem_limit_bytes=VMEM_BYTES
        ),
        name="exchange",
    )(
        send_species,
        send_cells,
        send_counts,
        grid_state,
        diff_rate.reshape(1, 16),
        prod_rate,
        loss_rate.reshape(1, 16),
        self_rate.reshape(1, 16),
    )

    lanes = min(capacity, 512)
    whole = lambda shape: pl.BlockSpec(shape, lambda g, k: (0,) * len(shape))
    return pl.pallas_call(
        react_kernel,
        grid=(devices // 16, capacity // lanes),
        out_shape=(
            jax.ShapeDtypeStruct(send_species.shape, f32),
            jax.ShapeDtypeStruct(grid_state.shape, f32),
        ),
        in_specs=[
            pl.BlockSpec((16, 16, lanes), lambda g, k: (g, 0, k)),
            pl.BlockSpec((16, 1, lanes), lambda g, k: (g, 0, k)),
            whole((4, 8, 16, 128)),
            whole((272, LOW)),
            whole((256, 256)),
            whole((2, 128, 128)),
        ],
        out_specs=(
            pl.BlockSpec((16, 16, lanes), lambda g, k: (g, 0, k)),
            whole(grid_state.shape),
        ),
        scratch_shapes=[pltpu.VMEM((256, LOW), bf16), pltpu.VMEM((16, 16, lanes), f32)],
        compiler_params=pltpu.CompilerParams(vmem_limit_bytes=VMEM_BYTES),
        name="react",
    )(arrived, cells, diffused, deposit, weight, rates)


def solution(mesh):
    placed = (
        P(("lon", "lat"), None, None),
        P(("lon", "lat"), None),
        P(("lon", "lat")),
        P(None, None, "lon", "lat"),
        P(),
        P(),
        P(),
        P(),
    )
    return jax.shard_map(
        local,
        mesh=mesh,
        in_specs=placed,
        out_specs=(P(("lon", "lat"), None, None), P(None, None, "lon", "lat")),
        check_vma=False,
    )
```

```python
import functools

import jax
import jax.numpy as jnp
from jax import lax
from jax.experimental import pallas as pl
from jax.experimental.pallas import tpu as pltpu
from jax.sharding import PartitionSpec as P

ITERS = 4
LOW = 256
WINDOW = 8
LANES = 512
VMEM_BYTES = 62 * 1024 * 1024

grid_weight = 0.5
parcel_pull = 0.3

f32 = jnp.float32
bf16 = jnp.bfloat16
MESH = pl.DeviceIdType.MESH


def hot_rows(index_row, count):
    wide = jnp.broadcast_to(index_row.astype(f32), (16, index_row.shape[1])).astype(bf16)
    rows = lax.broadcasted_iota(jnp.int32, (16, index_row.shape[1]), 0).astype(f32).astype(bf16)
    one = jnp.ones_like(wide)
    zero = jnp.zeros_like(wide)
    return jnp.concatenate(
        [jnp.where(wide == rows + float(16 * g), one, zero) for g in range(count // 16)], axis=0
    )


def step_kernel(
    n_lon,
    n_lat,
    species_hbm,
    cells_hbm,
    counts_hbm,
    grid_hbm,
    rate_hbm,
    prod_hbm,
    loss_hbm,
    self_hbm,
    parcels_hbm,
    mixed_ref,
    diffused_out,
    deposit_out,
    weight_out,
    rates_out,
    hot_out,
    coarse,
    cells_ref,
    counts_ref,
    grid_ref,
    rate_ref,
    prod_ref,
    loss_ref,
    self_ref,
    load_sem,
    arrived,
    marked,
    cells_in,
    field,
    east_halo,
    west_halo,
    north_halo,
    south_halo,
    edges,
    send_sem,
    recv_sem,
    send_cell_sem,
    recv_cell_sem,
    out_sem,
    halo_send,
    halo_recv,
):
    devices = n_lon * n_lat
    species_count = 16
    capacity = cells_ref.shape[1]
    lon = lax.axis_index("lon")
    lat = lax.axis_index("lat")
    me = lon * n_lat + lat

    def partner(step, sign):
        a = step // n_lat
        past = (a + n_lon - 1) // n_lon
        to_lon = lax.rem(lon + sign * a + n_lon, n_lon)
        source_lon = lon if sign > 0 else to_lon
        b = lax.rem(step + (n_lat // 2) * past * lax.rem(source_lon, 2), n_lat)
        to_lat = lax.rem(lat + sign * b + n_lat, n_lat)
        return to_lon, to_lat, to_lon * n_lat + to_lat

    loads = [
        pltpu.make_async_copy(source, target, load_sem.at[k])
        for k, (source, target) in enumerate(
            (
                (cells_hbm, cells_ref),
                (counts_hbm, counts_ref),
                (grid_hbm, grid_ref),
                (rate_hbm, rate_ref),
                (prod_hbm, prod_ref),
                (loss_hbm, loss_ref),
                (self_hbm, self_ref),
            )
        )
    ]
    for load in loads:
        load.start()
    barrier = pltpu.get_barrier_semaphore()

    def greet(step, carry):
        to_lon, to_lat, _ = partner(step, 1)
        pl.semaphore_signal(barrier, inc=1, device_id=(to_lon, to_lat), device_id_type=MESH)
        return carry

    lax.fori_loop(1, devices, greet, 0)

    own = pltpu.make_async_copy(species_hbm.at[me], arrived.at[me], recv_sem.at[me])
    own.start()

    loads[0].wait()
    loads[1].wait()
    slot = lax.broadcasted_iota(jnp.int32, (1, capacity), 1)

    def mark(row, carry):
        marked[row] = jnp.where(slot < counts_ref[row], cells_ref[pl.ds(row, 1), :], -1)
        return carry

    lax.fori_loop(0, devices, mark, 0)
    pl.semaphore_wait(barrier, devices - 1)

    def species_copy(to_lon, to_lat, tile):
        return pltpu.make_async_remote_copy(
            src_ref=species_hbm.at[tile],
            dst_ref=arrived.at[me],
            send_sem=send_sem.at[tile],
            recv_sem=recv_sem.at[me],
            device_id=(to_lon, to_lat),
            device_id_type=MESH,
        )

    def cells_copy(to_lon, to_lat, tile):
        return pltpu.make_async_remote_copy(
            src_ref=marked.at[tile],
            dst_ref=cells_in.at[me],
            send_sem=send_cell_sem.at[tile],
            recv_sem=recv_cell_sem.at[me],
            device_id=(to_lon, to_lat),
            device_id_type=MESH,
        )

    def send(step):
        to_lon, to_lat, tile = partner(step, 1)
        cells_copy(to_lon, to_lat, tile).start()
        species_copy(to_lon, to_lat, tile).start()

    def send_step(step, carry):
        send(step)
        return carry

    lax.fori_loop(1, WINDOW + 1, send_step, 0)
    for load in loads[2:]:
        load.wait()

    for j in range(4):
        for level in range(8):
            field[0, j, level] = grid_ref[:, level, j, :]

    def halo_copies(turn):
        up_lon = lax.rem(lon + 1, n_lon)
        down_lon = lax.rem(lon + n_lon - 1, n_lon)
        up_lat = lax.rem(lat + 1, n_lat)
        down_lat = lax.rem(lat + n_lat - 1, n_lat)
        plan = (
            (field.at[turn, 0], east_halo.at[turn], (down_lon, lat)),
            (field.at[turn, 3], west_halo.at[turn], (up_lon, lat)),
            (edges.at[turn, 0], north_halo.at[turn], (lon, down_lat)),
            (edges.at[turn, 1], south_halo.at[turn], (lon, up_lat)),
        )
        return [
            pltpu.make_async_remote_copy(
                src_ref=source,
                dst_ref=target,
                send_sem=halo_send.at[turn, k],
                recv_sem=halo_recv.at[turn, k],
                device_id=device,
                device_id_type=MESH,
            )
            for k, (source, target, device) in enumerate(plan)
        ]

    def halo_start(turn):
        edges[turn] = jnp.zeros_like(edges[turn])
        for j in range(4):
            turned = field[turn, j].reshape(128, 128).T
            edges[turn, 0, j : j + 1, :] = turned[0:1, :]
            edges[turn, 1, j : j + 1, :] = turned[127:128, :]
        for copy in halo_copies(turn):
            copy.start()

    def column(row, lane_count):
        pick = lax.broadcasted_iota(jnp.int32, (16, 16), 0) == lax.broadcasted_iota(
            jnp.int32, (16, 16), 1
        )
        return jnp.broadcast_to(
            jnp.sum(jnp.where(pick, row, 0.0), axis=1, keepdims=True), (16, lane_count)
        )

    rate = column(rate_ref[...], 128)
    lane = lax.broadcasted_iota(jnp.int32, (128, 128), 1)

    def diffuse(turn, store):
        for copy in halo_copies(turn):
            copy.wait()
        north_cols = north_halo[turn].T
        south_cols = south_halo[turn].T
        for j in range(4):
            v = field[turn, j].reshape(128, 128)
            east = east_halo[turn] if j == 3 else field[turn, j + 1]
            west = west_halo[turn] if j == 0 else field[turn, j - 1]
            north_col = jnp.broadcast_to(north_cols[:, j : j + 1], (128, 128))
            south_col = jnp.broadcast_to(south_cols[:, j : j + 1], (128, 128))
            north_edge = jnp.where(lat == n_lat - 1, v, north_col)
            south_edge = jnp.where(lat == 0, v, south_col)
            north = jnp.where(lane == 127, north_edge, pltpu.roll(v, 127, 1))
            south = jnp.where(lane == 0, south_edge, pltpu.roll(v, 1, 1))
            above = jnp.concatenate([v[16:], v[112:]], axis=0)
            below = jnp.concatenate([v[:16], v[:112]], axis=0)
            laplace = (
                east.reshape(128, 128)
                + west.reshape(128, 128)
                + north
                + south
                + above
                + below
                - 6.0 * v
            )
            store(j, (v + jnp.concatenate([rate] * 8, axis=0) * laplace).reshape(8, 16, 128))

    def store_field(j, value):
        field[1, j] = value

    def store_out(j, value):
        diffused_out[j] = value

    def deposit(tile):
        cells = cells_in[tile]
        rounded = arrived[tile].astype(bf16)
        low_hot = hot_rows(lax.bitwise_and(cells, LOW - 1), LOW)
        high = jnp.broadcast_to(lax.shift_right_arithmetic(cells, 8).astype(f32), (16, capacity))
        high = high.astype(bf16)
        zero = jnp.zeros_like(rounded)
        rows = lax.broadcasted_iota(jnp.int32, (16, capacity), 0).astype(f32).astype(bf16)
        spread = jnp.concatenate(
            [jnp.where(high == float(h), rounded, zero) for h in range(16)]
            + [jnp.where(high == rows, jnp.ones_like(zero), zero)],
            axis=0,
        )
        hot_out[tile] = low_hot
        deposit_out[...] += lax.dot_general(
            spread, low_hot, (((1,), (1,)), ((), ())), preferred_element_type=f32
        )

    def receive(step):
        from_lon, from_lat, tile = partner(step, -1)
        pltpu.make_async_remote_copy(
            src_ref=marked.at[tile],
            dst_ref=cells_in.at[tile],
            send_sem=send_cell_sem.at[tile],
            recv_sem=recv_cell_sem.at[tile],
            device_id=(from_lon, from_lat),
            device_id_type=MESH,
        ).wait_recv()
        pltpu.make_async_remote_copy(
            src_ref=species_hbm.at[tile],
            dst_ref=arrived.at[tile],
            send_sem=send_sem.at[tile],
            recv_sem=recv_sem.at[tile],
            device_id=(from_lon, from_lat),
            device_id_type=MESH,
        ).wait_recv()
        deposit(tile)

    def receive_send(step, carry):
        receive(step)

        @pl.when(step + WINDOW < devices)
        def refill():
            send(step + WINDOW)

        return carry

    halo_start(0)

    spot = lax.broadcasted_iota(jnp.int32, (256, 16), 0)
    spots = lax.broadcasted_iota(jnp.int32, (256, 16), 1)
    tall = jnp.where(lax.rem(spot, 16) == spots, 1.0, 0.0).astype(bf16)
    prod = prod_ref[...]
    prod_hi = prod.astype(bf16)
    prod_lo = (prod - prod_hi.astype(f32)).astype(bf16)
    row = lax.broadcasted_iota(jnp.int32, (256, 256), 0)
    col = lax.broadcasted_iota(jnp.int32, (256, 256), 1)
    same = lax.rem(row // 16, 8) == lax.rem(col // 16, 8)
    wide = []
    for part in (prod_hi, prod_lo):
        half = jnp.dot(tall, part, preferred_element_type=f32).astype(bf16)
        wide.append(
            lax.dot_general(half, tall, (((1,), (1,)), ((), ())), preferred_element_type=f32)
        )
    weight_out[...] = jnp.where(
        same, jnp.where(row < 128, wide[0], jnp.where(col < 128, wide[1], 0.0)), 0.0
    ).astype(bf16)
    rates_out[0] = jnp.concatenate([1.0 + column(loss_ref[...], 128)] * 8, axis=0)
    rates_out[1] = jnp.concatenate([column(self_ref[...], 128)] * 8, axis=0)

    deposit_out[...] = jnp.zeros_like(deposit_out)
    cells_in[me] = marked[me]
    own.wait()
    deposit(me)

    first = devices // 4
    second = devices // 2
    lax.fori_loop(1, first, receive_send, 0)
    diffuse(0, store_field)
    halo_start(1)
    lax.fori_loop(first, second, receive_send, 0)
    diffuse(1, store_out)
    lax.fori_loop(second, devices, receive_send, 0)

    for h in range(16):
        for side in range(2):
            lanes = slice(128 * side, 128 * (side + 1))
            j = 2 * (h % 2) + side
            number = deposit_out[256 + h : 257 + h, lanes]
            value = (
                diffused_out[j, h // 2] + grid_weight * deposit_out[16 * h : 16 * (h + 1), lanes]
            ) / (1.0 + grid_weight * number)
            mixed_ref[:, h // 2, j, :] = value
            coarse[16 * h : 16 * (h + 1), lanes] = value.astype(bf16)

    chunk = min(capacity, 256)
    chunks = [slice(k, k + chunk) for k in range(0, capacity, chunk)]

    def blend(tile, carry):
        for where in chunks:
            cells = cells_in[tile, :, where]
            picked = jnp.dot(coarse[...], hot_out[tile, :, where], preferred_element_type=f32)
            high = jnp.broadcast_to(lax.shift_right_arithmetic(cells, 8), (16, chunk))
            found = picked[:16]
            for h in range(1, 16):
                found = jnp.where(high == h, picked[16 * h : 16 * (h + 1)], found)
            start = arrived[tile, :, where]
            arrived[tile, :, where] = start + parcel_pull * (found - start)
        return carry

    lanes = min(capacity, LANES)
    parts_of = capacity // lanes
    loss = jnp.concatenate([rates_out[0]] * (chunk // 128), axis=1)
    self_loss = jnp.concatenate([rates_out[1]] * (chunk // 128), axis=1)

    def out_copy(turn):
        tiles = pl.ds(16 * (turn // parts_of), 16)
        where = pl.ds(pl.multiple_of(lax.rem(turn, parts_of) * lanes, 128), lanes)
        return pltpu.make_async_copy(
            arrived.at[tiles, :, where], parcels_hbm.at[tiles, :, where], out_sem.at[turn]
        )

    def react(turn, carry):
        tile = 16 * (turn // parts_of)
        base = lax.rem(turn, parts_of) * lanes
        groups = [
            (tile + first, pl.ds(pl.multiple_of(base + k, 128), chunk))
            for k in range(0, lanes, chunk)
            for first in (0, 8)
        ]
        starts = [
            arrived[pl.ds(first, 8), :, where].reshape(128, chunk) for first, where in groups
        ]
        states = starts
        for sweep in range(ITERS):
            parts = []
            for state in states:
                high_part = state.astype(bf16)
                low_part = (state - high_part.astype(f32)).astype(bf16)
                parts.append(jnp.concatenate([high_part, low_part], axis=0))
            products = [
                jnp.dot(weight_out[...], part, preferred_element_type=f32) for part in parts
            ]
            later = []
            for start, state, product in zip(starts, states, products):
                produced = start + (product[:128] + product[128:])
                bottom = loss + self_loss * state
                inverse = pl.reciprocal(bottom, approx=True)
                later.append(produced * (inverse * (2.0 - bottom * inverse)))
            states = later
        for (first, where), state in zip(groups, states):
            for k in range(8):
                alive = jnp.broadcast_to(cells_in[first + k, :, where] >= 0, (16, chunk))
                arrived[first + k, :, where] = jnp.where(
                    alive, state[16 * k : 16 * (k + 1)], 0.0
                )
        out_copy(turn).start()
        return carry

    def group_of_tiles(group, carry):
        lax.fori_loop(16 * group, 16 * (group + 1), blend, 0)
        lax.fori_loop(group * parts_of, (group + 1) * parts_of, react, 0)
        return carry

    lax.fori_loop(0, devices // 16, group_of_tiles, 0)

    def finish(step, carry):
        to_lon, to_lat, tile = partner(step, 1)
        cells_copy(to_lon, to_lat, tile).wait_send()
        species_copy(to_lon, to_lat, tile).wait_send()
        return carry

    lax.fori_loop(1, devices, finish, 0)

    def finish_out(turn, carry):
        out_copy(turn).wait()
        return carry

    lax.fori_loop(0, devices // 16 * parts_of, finish_out, 0)


def local(
    send_species, send_cells, send_counts, grid_state, diff_rate, prod_rate, loss_rate, self_rate
):
    n_lon = lax.axis_size("lon")
    n_lat = lax.axis_size("lat")
    devices, species_count, capacity = send_species.shape
    hbm = pl.BlockSpec(memory_space=pl.ANY)
    return pl.pallas_call(
        functools.partial(step_kernel, n_lon, n_lat),
        out_shape=(
            jax.ShapeDtypeStruct(send_species.shape, f32),
            jax.ShapeDtypeStruct(grid_state.shape, f32),
        ),
        in_specs=[hbm] * 8,
        out_specs=(hbm, pl.BlockSpec(memory_space=pltpu.VMEM)),
        scratch_shapes=[
            pltpu.VMEM((4, 8, 16, 128), f32),
            pltpu.VMEM((272, LOW), f32),
            pltpu.VMEM((256, 256), bf16),
            pltpu.VMEM((2, 128, 128), f32),
            pltpu.VMEM((devices, LOW, capacity), bf16),
            pltpu.VMEM((256, LOW), bf16),
            pltpu.VMEM(send_cells.shape, jnp.int32),
            pltpu.SMEM(send_counts.shape, jnp.int32),
            pltpu.VMEM(grid_state.shape, f32),
            pltpu.VMEM((1, 16), f32),
            pltpu.VMEM((16, 16), f32),
            pltpu.VMEM((1, 16), f32),
            pltpu.VMEM((1, 16), f32),
            pltpu.SemaphoreType.DMA((7,)),
            pltpu.VMEM((devices, species_count, capacity), f32),
            pltpu.VMEM((devices, 1, capacity), jnp.int32),
            pltpu.VMEM((devices, 1, capacity), jnp.int32),
            pltpu.VMEM((2, 4, 8, 16, 128), f32),
            pltpu.VMEM((2, 8, 16, 128), f32),
            pltpu.VMEM((2, 8, 16, 128), f32),
            pltpu.VMEM((2, 8, 128), f32),
            pltpu.VMEM((2, 8, 128), f32),
            pltpu.VMEM((2, 2, 8, 128), f32),
            pltpu.SemaphoreType.DMA((devices,)),
            pltpu.SemaphoreType.DMA((devices,)),
            pltpu.SemaphoreType.DMA((devices,)),
            pltpu.SemaphoreType.DMA((devices,)),
            pltpu.SemaphoreType.DMA((devices // 16 * (capacity // min(capacity, LANES)),)),
            pltpu.SemaphoreType.DMA((2, 4)),
            pltpu.SemaphoreType.DMA((2, 4)),
        ],
        compiler_params=pltpu.CompilerParams(
            collective_id=0, has_side_effects=True, vmem_limit_bytes=VMEM_BYTES
        ),
        name="step",
    )(
        send_species,
        send_cells,
        send_counts,
        grid_state,
        diff_rate.reshape(1, 16),
        prod_rate,
        loss_rate.reshape(1, 16),
        self_rate.reshape(1, 16),
    )


def solution(mesh):
    placed = (
        P(("lon", "lat"), None, None),
        P(("lon", "lat"), None),
        P(("lon", "lat")),
        P(None, None, "lon", "lat"),
        P(),
        P(),
        P(),
        P(),
    )
    return jax.shard_map(
        local,
        mesh=mesh,
        in_specs=placed,
        out_specs=(P(("lon", "lat"), None, None), P(None, None, "lon", "lat")),
        check_vma=False,
    )
```

```python
import functools

import jax
import jax.numpy as jnp
from jax import lax
from jax.experimental import pallas as pl
from jax.experimental.pallas import tpu as pltpu
from jax.sharding import PartitionSpec as P

ITERS = 4
LOW = 256
WINDOW = 8
VMEM_BYTES = 62 * 1024 * 1024

grid_weight = 0.5
parcel_pull = 0.3

f32 = jnp.float32
bf16 = jnp.bfloat16
MESH = pl.DeviceIdType.MESH


def hot_rows(index_row, count):
    wide = jnp.broadcast_to(index_row.astype(f32), (16, index_row.shape[1])).astype(bf16)
    rows = lax.broadcasted_iota(jnp.int32, (16, index_row.shape[1]), 0).astype(f32).astype(bf16)
    one = jnp.ones_like(wide)
    zero = jnp.zeros_like(wide)
    return jnp.concatenate(
        [jnp.where(wide == rows + float(16 * g), one, zero) for g in range(count // 16)], axis=0
    )


def exchange_kernel(
    n_lon,
    n_lat,
    species_hbm,
    cells_hbm,
    counts_hbm,
    grid_hbm,
    rate_hbm,
    prod_hbm,
    loss_hbm,
    self_hbm,
    arrived_out,
    cells_out,
    diffused_out,
    deposit_out,
    weight_out,
    rates_out,
    cells_ref,
    counts_ref,
    grid_ref,
    rate_ref,
    prod_ref,
    loss_ref,
    self_ref,
    load_sem,
    arrived,
    marked,
    cells_in,
    field,
    east_halo,
    west_halo,
    north_halo,
    south_halo,
    edges,
    send_sem,
    recv_sem,
    send_cell_sem,
    recv_cell_sem,
    out_sem,
    out_cell_sem,
    halo_send,
    halo_recv,
):
    devices = n_lon * n_lat
    species_count = 16
    capacity = cells_ref.shape[1]
    lon = lax.axis_index("lon")
    lat = lax.axis_index("lat")
    me = lon * n_lat + lat

    def partner(step, sign):
        a = step // n_lat
        past = (a + n_lon - 1) // n_lon
        to_lon = lax.rem(lon + sign * a + n_lon, n_lon)
        source_lon = lon if sign > 0 else to_lon
        b = lax.rem(step + (n_lat // 2) * past * lax.rem(source_lon, 2), n_lat)
        to_lat = lax.rem(lat + sign * b + n_lat, n_lat)
        return to_lon, to_lat, to_lon * n_lat + to_lat

    loads = [
        pltpu.make_async_copy(source, target, load_sem.at[k])
        for k, (source, target) in enumerate(
            (
                (cells_hbm, cells_ref),
                (counts_hbm, counts_ref),
                (grid_hbm, grid_ref),
                (rate_hbm, rate_ref),
                (prod_hbm, prod_ref),
                (loss_hbm, loss_ref),
                (self_hbm, self_ref),
            )
        )
    ]
    for load in loads:
        load.start()
    barrier = pltpu.get_barrier_semaphore()

    def greet(step, carry):
        to_lon, to_lat, _ = partner(step, 1)
        pl.semaphore_signal(barrier, inc=1, device_id=(to_lon, to_lat), device_id_type=MESH)
        return carry

    lax.fori_loop(1, devices, greet, 0)

    own = pltpu.make_async_copy(species_hbm.at[me], arrived.at[me], recv_sem.at[me])
    own.start()

    loads[0].wait()
    loads[1].wait()
    slot = lax.broadcasted_iota(jnp.int32, (1, capacity), 1)

    def mark(row, carry):
        marked[row] = jnp.where(slot < counts_ref[row], cells_ref[pl.ds(row, 1), :], -1)
        return carry

    lax.fori_loop(0, devices, mark, 0)
    pl.semaphore_wait(barrier, devices - 1)

    def species_copy(to_lon, to_lat, tile):
        return pltpu.make_async_remote_copy(
            src_ref=species_hbm.at[tile],
            dst_ref=arrived.at[me],
            send_sem=send_sem.at[tile],
            recv_sem=recv_sem.at[me],
            device_id=(to_lon, to_lat),
            device_id_type=MESH,
        )

    def cells_copy(to_lon, to_lat, tile):
        return pltpu.make_async_remote_copy(
            src_ref=marked.at[tile],
            dst_ref=cells_in.at[me],
            send_sem=send_cell_sem.at[tile],
            recv_sem=recv_cell_sem.at[me],
            device_id=(to_lon, to_lat),
            device_id_type=MESH,
        )

    def send(step):
        to_lon, to_lat, tile = partner(step, 1)
        cells_copy(to_lon, to_lat, tile).start()
        species_copy(to_lon, to_lat, tile).start()

    def send_step(step, carry):
        send(step)
        return carry

    lax.fori_loop(1, WINDOW + 1, send_step, 0)
    for load in loads[2:]:
        load.wait()

    for j in range(4):
        for level in range(8):
            field[0, j, level] = grid_ref[:, level, j, :]

    def halo_copies(turn):
        up_lon = lax.rem(lon + 1, n_lon)
        down_lon = lax.rem(lon + n_lon - 1, n_lon)
        up_lat = lax.rem(lat + 1, n_lat)
        down_lat = lax.rem(lat + n_lat - 1, n_lat)
        plan = (
            (field.at[turn, 0], east_halo.at[turn], (down_lon, lat)),
            (field.at[turn, 3], west_halo.at[turn], (up_lon, lat)),
            (edges.at[turn, 0], north_halo.at[turn], (lon, down_lat)),
            (edges.at[turn, 1], south_halo.at[turn], (lon, up_lat)),
        )
        return [
            pltpu.make_async_remote_copy(
                src_ref=source,
                dst_ref=target,
                send_sem=halo_send.at[turn, k],
                recv_sem=halo_recv.at[turn, k],
                device_id=device,
                device_id_type=MESH,
            )
            for k, (source, target, device) in enumerate(plan)
        ]

    def halo_start(turn):
        edges[turn] = jnp.zeros_like(edges[turn])
        for j in range(4):
            turned = field[turn, j].reshape(128, 128).T
            edges[turn, 0, j : j + 1, :] = turned[0:1, :]
            edges[turn, 1, j : j + 1, :] = turned[127:128, :]
        for copy in halo_copies(turn):
            copy.start()

    def column(row, lane_count):
        pick = lax.broadcasted_iota(jnp.int32, (16, 16), 0) == lax.broadcasted_iota(
            jnp.int32, (16, 16), 1
        )
        return jnp.broadcast_to(
            jnp.sum(jnp.where(pick, row, 0.0), axis=1, keepdims=True), (16, lane_count)
        )

    rate = column(rate_ref[...], 128)
    lane = lax.broadcasted_iota(jnp.int32, (128, 128), 1)

    def diffuse(turn, store):
        for copy in halo_copies(turn):
            copy.wait()
        north_cols = north_halo[turn].T
        south_cols = south_halo[turn].T
        for j in range(4):
            v = field[turn, j].reshape(128, 128)
            east = east_halo[turn] if j == 3 else field[turn, j + 1]
            west = west_halo[turn] if j == 0 else field[turn, j - 1]
            north_col = jnp.broadcast_to(north_cols[:, j : j + 1], (128, 128))
            south_col = jnp.broadcast_to(south_cols[:, j : j + 1], (128, 128))
            north_edge = jnp.where(lat == n_lat - 1, v, north_col)
            south_edge = jnp.where(lat == 0, v, south_col)
            north = jnp.where(lane == 127, north_edge, pltpu.roll(v, 127, 1))
            south = jnp.where(lane == 0, south_edge, pltpu.roll(v, 1, 1))
            above = jnp.concatenate([v[16:], v[112:]], axis=0)
            below = jnp.concatenate([v[:16], v[:112]], axis=0)
            laplace = (
                east.reshape(128, 128)
                + west.reshape(128, 128)
                + north
                + south
                + above
                + below
                - 6.0 * v
            )
            store(j, (v + jnp.concatenate([rate] * 8, axis=0) * laplace).reshape(8, 16, 128))

    def store_field(j, value):
        field[1, j] = value

    def store_out(j, value):
        diffused_out[j] = value

    def deposit(tile):
        cells = cells_in[tile]
        rounded = arrived[tile].astype(bf16)
        low_hot = hot_rows(lax.bitwise_and(cells, LOW - 1), LOW)
        high = jnp.broadcast_to(lax.shift_right_arithmetic(cells, 8).astype(f32), (16, capacity))
        high = high.astype(bf16)
        zero = jnp.zeros_like(rounded)
        rows = lax.broadcasted_iota(jnp.int32, (16, capacity), 0).astype(f32).astype(bf16)
        spread = jnp.concatenate(
            [jnp.where(high == float(h), rounded, zero) for h in range(16)]
            + [jnp.where(high == rows, jnp.ones_like(zero), zero)],
            axis=0,
        )
        deposit_out[...] += lax.dot_general(
            spread, low_hot, (((1,), (1,)), ((), ())), preferred_element_type=f32
        )

    def keep(tile):
        pltpu.make_async_copy(arrived.at[tile], arrived_out.at[tile], out_sem.at[tile]).start()
        pltpu.make_async_copy(cells_in.at[tile], cells_out.at[tile], out_cell_sem.at[tile]).start()

    def receive(step, carry):
        from_lon, from_lat, tile = partner(step, -1)
        pltpu.make_async_remote_copy(
            src_ref=marked.at[tile],
            dst_ref=cells_in.at[tile],
            send_sem=send_cell_sem.at[tile],
            recv_sem=recv_cell_sem.at[tile],
            device_id=(from_lon, from_lat),
            device_id_type=MESH,
        ).wait_recv()
        pltpu.make_async_remote_copy(
            src_ref=species_hbm.at[tile],
            dst_ref=arrived.at[tile],
            send_sem=send_sem.at[tile],
            recv_sem=recv_sem.at[tile],
            device_id=(from_lon, from_lat),
            device_id_type=MESH,
        ).wait_recv()
        keep(tile)
        deposit(tile)
        return carry

    def receive_send(step, carry):
        receive(step, carry)

        @pl.when(step + WINDOW < devices)
        def refill():
            send(step + WINDOW)

        return carry

    halo_start(0)

    spot = lax.broadcasted_iota(jnp.int32, (256, 16), 0)
    spots = lax.broadcasted_iota(jnp.int32, (256, 16), 1)
    tall = jnp.where(lax.rem(spot, 16) == spots, 1.0, 0.0).astype(bf16)
    prod = prod_ref[...]
    prod_hi = prod.astype(bf16)
    prod_lo = (prod - prod_hi.astype(f32)).astype(bf16)
    row = lax.broadcasted_iota(jnp.int32, (256, 256), 0)
    col = lax.broadcasted_iota(jnp.int32, (256, 256), 1)
    same = lax.rem(row // 16, 8) == lax.rem(col // 16, 8)
    wide = []
    for part in (prod_hi, prod_lo):
        half = jnp.dot(tall, part, preferred_element_type=f32).astype(bf16)
        wide.append(
            lax.dot_general(half, tall, (((1,), (1,)), ((), ())), preferred_element_type=f32)
        )
    weight_out[...] = jnp.where(
        same, jnp.where(row < 128, wide[0], jnp.where(col < 128, wide[1], 0.0)), 0.0
    ).astype(bf16)
    rates_out[0] = jnp.concatenate([1.0 + column(loss_ref[...], 128)] * 8, axis=0)
    rates_out[1] = jnp.concatenate([column(self_ref[...], 128)] * 8, axis=0)

    deposit_out[...] = jnp.zeros_like(deposit_out)
    cells_in[me] = marked[me]
    own.wait()
    keep(me)
    deposit(me)

    first = devices // 4
    second = devices // 2
    lax.fori_loop(1, first, receive_send, 0)
    diffuse(0, store_field)
    halo_start(1)
    lax.fori_loop(first, second, receive_send, 0)
    diffuse(1, store_out)
    lax.fori_loop(second, devices, receive_send, 0)

    def finish(step, carry):
        to_lon, to_lat, tile = partner(step, 1)
        cells_copy(to_lon, to_lat, tile).wait_send()
        species_copy(to_lon, to_lat, tile).wait_send()
        return carry

    lax.fori_loop(1, devices, finish, 0)

    def finish_keep(tile, carry):
        pltpu.make_async_copy(arrived.at[tile], arrived_out.at[tile], out_sem.at[tile]).wait()
        pltpu.make_async_copy(cells_in.at[tile], cells_out.at[tile], out_cell_sem.at[tile]).wait()
        return carry

    lax.fori_loop(0, devices, finish_keep, 0)


def react_kernel(
    arrived_ref,
    cells_ref,
    diffused_ref,
    deposit_ref,
    weight_ref,
    rates_ref,
    parcels_ref,
    mixed_ref,
    coarse,
    blended,
):
    @pl.when((pl.program_id(0) == 0) & (pl.program_id(1) == 0))
    def mix():
        for h in range(16):
            for side in range(2):
                lanes = slice(128 * side, 128 * (side + 1))
                j = 2 * (h % 2) + side
                number = deposit_ref[256 + h : 257 + h, lanes]
                value = (
                    diffused_ref[j, h // 2]
                    + grid_weight * deposit_ref[16 * h : 16 * (h + 1), lanes]
                ) / (1.0 + grid_weight * number)
                mixed_ref[:, h // 2, j, :] = value
                coarse[16 * h : 16 * (h + 1), lanes] = value.astype(bf16)

    lanes = arrived_ref.shape[2]
    chunk = min(lanes, 256)
    chunks = [slice(k, k + chunk) for k in range(0, lanes, chunk)]
    loss = jnp.concatenate([rates_ref[0]] * (chunk // 128), axis=1)
    self_loss = jnp.concatenate([rates_ref[1]] * (chunk // 128), axis=1)

    def blend(source, carry):
        for where in chunks:
            cells = cells_ref[source, :, where]
            low_hot = hot_rows(lax.bitwise_and(cells, LOW - 1), LOW)
            picked = jnp.dot(coarse[...], low_hot, preferred_element_type=f32)
            high = jnp.broadcast_to(lax.shift_right_arithmetic(cells, 8), (8, chunk))
            upper, lower = picked[:8], picked[8:16]
            for h in range(1, 16):
                here = high == h
                upper = jnp.where(here, picked[16 * h : 16 * h + 8], upper)
                lower = jnp.where(here, picked[16 * h + 8 : 16 * h + 16], lower)
            found = jnp.concatenate([upper, lower], axis=0)
            start = arrived_ref[source, :, where]
            blended[source, :, where] = start + parcel_pull * (found - start)
        return carry

    lax.fori_loop(0, 16, blend, 0, unroll=8)

    groups = [(first, where) for where in chunks for first in (0, 8)]
    starts = [
        blended[first : first + 8, :, where].reshape(128, chunk) for first, where in groups
    ]
    states = starts
    for sweep in range(ITERS):
        parts = []
        for state in states:
            high_part = state.astype(bf16)
            low_part = (state - high_part.astype(f32)).astype(bf16)
            parts.append(jnp.concatenate([high_part, low_part], axis=0))
        products = [jnp.dot(weight_ref[...], part, preferred_element_type=f32) for part in parts]
        later = []
        for start, state, product in zip(starts, states, products):
            produced = start + (product[:128] + product[128:])
            bottom = loss + self_loss * state
            inverse = pl.reciprocal(bottom, approx=True)
            later.append(produced * (inverse * (2.0 - bottom * inverse)))
        states = later
    for (first, where), state in zip(groups, states):
        for k in range(8):
            alive = jnp.broadcast_to(cells_ref[first + k, :, where] >= 0, (16, chunk))
            parcels_ref[first + k, :, where] = jnp.where(
                alive, state[16 * k : 16 * (k + 1)], 0.0
            )


def local(
    send_species, send_cells, send_counts, grid_state, diff_rate, prod_rate, loss_rate, self_rate
):
    n_lon = lax.axis_size("lon")
    n_lat = lax.axis_size("lat")
    devices, species_count, capacity = send_species.shape
    vmem = pl.BlockSpec(memory_space=pltpu.VMEM)
    hbm = pl.BlockSpec(memory_space=pl.ANY)
    arrived, cells, diffused, deposit, weight, rates = pl.pallas_call(
        functools.partial(exchange_kernel, n_lon, n_lat),
        out_shape=(
            jax.ShapeDtypeStruct((devices, species_count, capacity), f32),
            jax.ShapeDtypeStruct((devices, 1, capacity), jnp.int32),
            jax.ShapeDtypeStruct((4, 8, 16, 128), f32),
            jax.ShapeDtypeStruct((272, LOW), f32),
            jax.ShapeDtypeStruct((256, 256), bf16),
            jax.ShapeDtypeStruct((2, 128, 128), f32),
        ),
        in_specs=[pl.BlockSpec(memory_space=pltpu.HBM)] * 8,
        out_specs=(hbm, hbm, vmem, vmem, vmem, vmem),
        scratch_shapes=[
            pltpu.VMEM(send_cells.shape, jnp.int32),
            pltpu.SMEM(send_counts.shape, jnp.int32),
            pltpu.VMEM(grid_state.shape, f32),
            pltpu.VMEM((1, 16), f32),
            pltpu.VMEM((16, 16), f32),
            pltpu.VMEM((1, 16), f32),
            pltpu.VMEM((1, 16), f32),
            pltpu.SemaphoreType.DMA((7,)),
            pltpu.VMEM((devices, species_count, capacity), f32),
            pltpu.VMEM((devices, 1, capacity), jnp.int32),
            pltpu.VMEM((devices, 1, capacity), jnp.int32),
            pltpu.VMEM((2, 4, 8, 16, 128), f32),
            pltpu.VMEM((2, 8, 16, 128), f32),
            pltpu.VMEM((2, 8, 16, 128), f32),
            pltpu.VMEM((2, 8, 128), f32),
            pltpu.VMEM((2, 8, 128), f32),
            pltpu.VMEM((2, 2, 8, 128), f32),
            pltpu.SemaphoreType.DMA((devices,)),
            pltpu.SemaphoreType.DMA((devices,)),
            pltpu.SemaphoreType.DMA((devices,)),
            pltpu.SemaphoreType.DMA((devices,)),
            pltpu.SemaphoreType.DMA((devices,)),
            pltpu.SemaphoreType.DMA((devices,)),
            pltpu.SemaphoreType.DMA((2, 4)),
            pltpu.SemaphoreType.DMA((2, 4)),
        ],
        compiler_params=pltpu.CompilerParams(
            collective_id=0, has_side_effects=True, vmem_limit_bytes=VMEM_BYTES
        ),
        name="exchange",
    )(
        send_species,
        send_cells,
        send_counts,
        grid_state,
        diff_rate.reshape(1, 16),
        prod_rate,
        loss_rate.reshape(1, 16),
        self_rate.reshape(1, 16),
    )

    lanes = min(capacity, 512)
    whole = lambda shape: pl.BlockSpec(shape, lambda g, k: (0,) * len(shape))
    return pl.pallas_call(
        react_kernel,
        grid=(devices // 16, capacity // lanes),
        out_shape=(
            jax.ShapeDtypeStruct(send_species.shape, f32),
            jax.ShapeDtypeStruct(grid_state.shape, f32),
        ),
        in_specs=[
            pl.BlockSpec((16, 16, lanes), lambda g, k: (g, 0, k)),
            pl.BlockSpec((16, 1, lanes), lambda g, k: (g, 0, k)),
            whole((4, 8, 16, 128)),
            whole((272, LOW)),
            whole((256, 256)),
            whole((2, 128, 128)),
        ],
        out_specs=(
            pl.BlockSpec((16, 16, lanes), lambda g, k: (g, 0, k)),
            whole(grid_state.shape),
        ),
        scratch_shapes=[pltpu.VMEM((256, LOW), bf16), pltpu.VMEM((16, 16, lanes), f32)],
        compiler_params=pltpu.CompilerParams(vmem_limit_bytes=VMEM_BYTES),
        name="react",
    )(arrived, cells, diffused, deposit, weight, rates)


def solution(mesh):
    placed = (
        P(("lon", "lat"), None, None),
        P(("lon", "lat"), None),
        P(("lon", "lat")),
        P(None, None, "lon", "lat"),
        P(),
        P(),
        P(),
        P(),
    )
    return jax.shard_map(
        local,
        mesh=mesh,
        in_specs=placed,
        out_specs=(P(("lon", "lat"), None, None), P(None, None, "lon", "lat")),
        check_vma=False,
    )
```

```python
import functools

import jax
import jax.numpy as jnp
from jax import lax
from jax.experimental import pallas as pl
from jax.experimental.pallas import tpu as pltpu
from jax.sharding import PartitionSpec as P

ITERS = 4
LOW = 256
WINDOW = 8
LAG = 2
CHUNK = 256
VMEM_BYTES = 62 * 1024 * 1024

grid_weight = 0.5
parcel_pull = 0.3

f32 = jnp.float32
bf16 = jnp.bfloat16
MESH = pl.DeviceIdType.MESH


def hot_rows(index_row, count):
    wide = jnp.broadcast_to(index_row.astype(f32), (16, index_row.shape[1])).astype(bf16)
    rows = lax.broadcasted_iota(jnp.int32, (16, index_row.shape[1]), 0).astype(f32).astype(bf16)
    one = jnp.ones_like(wide)
    zero = jnp.zeros_like(wide)
    return jnp.concatenate(
        [jnp.where(wide == rows + float(16 * g), one, zero) for g in range(count // 16)], axis=0
    )


def exchange_kernel(
    n_lon,
    n_lat,
    species_hbm,
    cells_hbm,
    counts_hbm,
    grid_hbm,
    rate_hbm,
    prod_hbm,
    loss_hbm,
    self_hbm,
    arrived_out,
    cells_out,
    diffused_out,
    deposit_out,
    weight_out,
    rates_out,
    cells_ref,
    counts_ref,
    grid_ref,
    rate_ref,
    prod_ref,
    loss_ref,
    self_ref,
    load_sem,
    arrived,
    marked,
    cells_in,
    field,
    east_halo,
    west_halo,
    north_halo,
    south_halo,
    edges,
    send_sem,
    recv_sem,
    send_cell_sem,
    recv_cell_sem,
    out_sem,
    out_cell_sem,
    halo_send,
    halo_recv,
):
    devices = n_lon * n_lat
    species_count = 16
    capacity = cells_ref.shape[1]
    lon = lax.axis_index("lon")
    lat = lax.axis_index("lat")
    me = lon * n_lat + lat

    def partner(step, sign):
        a = step // n_lat
        past = (a + n_lon - 1) // n_lon
        to_lon = lax.rem(lon + sign * a + n_lon, n_lon)
        source_lon = lon if sign > 0 else to_lon
        b = lax.rem(step + (n_lat // 2) * past * lax.rem(source_lon, 2), n_lat)
        to_lat = lax.rem(lat + sign * b + n_lat, n_lat)
        return to_lon, to_lat, to_lon * n_lat + to_lat

    loads = [
        pltpu.make_async_copy(source, target, load_sem.at[k])
        for k, (source, target) in enumerate(
            (
                (cells_hbm, cells_ref),
                (counts_hbm, counts_ref),
                (grid_hbm, grid_ref),
                (rate_hbm, rate_ref),
                (prod_hbm, prod_ref),
                (loss_hbm, loss_ref),
                (self_hbm, self_ref),
            )
        )
    ]
    for load in loads:
        load.start()
    barrier = pltpu.get_barrier_semaphore()

    def greet(step, carry):
        to_lon, to_lat, _ = partner(step, 1)
        pl.semaphore_signal(barrier, inc=1, device_id=(to_lon, to_lat), device_id_type=MESH)
        return carry

    lax.fori_loop(1, devices, greet, 0)

    own = pltpu.make_async_copy(species_hbm.at[me], arrived.at[me], recv_sem.at[me])
    own.start()

    loads[0].wait()
    loads[1].wait()
    slot = lax.broadcasted_iota(jnp.int32, (1, capacity), 1)

    def mark(row, carry):
        marked[row] = jnp.where(slot < counts_ref[row], cells_ref[pl.ds(row, 1), :], -1)
        return carry

    lax.fori_loop(0, devices, mark, 0)
    pl.semaphore_wait(barrier, devices - 1)

    def species_copy(to_lon, to_lat, tile):
        return pltpu.make_async_remote_copy(
            src_ref=species_hbm.at[tile],
            dst_ref=arrived.at[me],
            send_sem=send_sem.at[tile],
            recv_sem=recv_sem.at[me],
            device_id=(to_lon, to_lat),
            device_id_type=MESH,
        )

    def cells_copy(to_lon, to_lat, tile):
        return pltpu.make_async_remote_copy(
            src_ref=marked.at[tile],
            dst_ref=cells_in.at[me],
            send_sem=send_cell_sem.at[tile],
            recv_sem=recv_cell_sem.at[me],
            device_id=(to_lon, to_lat),
            device_id_type=MESH,
        )

    def send(step):
        to_lon, to_lat, tile = partner(step, 1)
        cells_copy(to_lon, to_lat, tile).start()
        species_copy(to_lon, to_lat, tile).start()

    def send_step(step, carry):
        send(step)
        return carry

    lax.fori_loop(1, WINDOW + 1, send_step, 0)
    for load in loads[2:]:
        load.wait()

    for j in range(4):
        for level in range(8):
            field[0, j, level] = grid_ref[:, level, j, :]

    def halo_copies(turn):
        up_lon = lax.rem(lon + 1, n_lon)
        down_lon = lax.rem(lon + n_lon - 1, n_lon)
        up_lat = lax.rem(lat + 1, n_lat)
        down_lat = lax.rem(lat + n_lat - 1, n_lat)
        plan = (
            (field.at[turn, 0], east_halo.at[turn], (down_lon, lat)),
            (field.at[turn, 3], west_halo.at[turn], (up_lon, lat)),
            (edges.at[turn, 0], north_halo.at[turn], (lon, down_lat)),
            (edges.at[turn, 1], south_halo.at[turn], (lon, up_lat)),
        )
        return [
            pltpu.make_async_remote_copy(
                src_ref=source,
                dst_ref=target,
                send_sem=halo_send.at[turn, k],
                recv_sem=halo_recv.at[turn, k],
                device_id=device,
                device_id_type=MESH,
            )
            for k, (source, target, device) in enumerate(plan)
        ]

    def halo_start(turn):
        edges[turn] = jnp.zeros_like(edges[turn])
        for j in range(4):
            turned = field[turn, j].reshape(128, 128).T
            edges[turn, 0, j : j + 1, :] = turned[0:1, :]
            edges[turn, 1, j : j + 1, :] = turned[127:128, :]
        for copy in halo_copies(turn):
            copy.start()

    def column(row, lane_count):
        pick = lax.broadcasted_iota(jnp.int32, (16, 16), 0) == lax.broadcasted_iota(
            jnp.int32, (16, 16), 1
        )
        return jnp.broadcast_to(
            jnp.sum(jnp.where(pick, row, 0.0), axis=1, keepdims=True), (16, lane_count)
        )

    rate = column(rate_ref[...], 128)
    lane = lax.broadcasted_iota(jnp.int32, (128, 128), 1)

    def diffuse(turn, store):
        for copy in halo_copies(turn):
            copy.wait()
        north_cols = north_halo[turn].T
        south_cols = south_halo[turn].T
        for j in range(4):
            v = field[turn, j].reshape(128, 128)
            east = east_halo[turn] if j == 3 else field[turn, j + 1]
            west = west_halo[turn] if j == 0 else field[turn, j - 1]
            north_col = jnp.broadcast_to(north_cols[:, j : j + 1], (128, 128))
            south_col = jnp.broadcast_to(south_cols[:, j : j + 1], (128, 128))
            north_edge = jnp.where(lat == n_lat - 1, v, north_col)
            south_edge = jnp.where(lat == 0, v, south_col)
            north = jnp.where(lane == 127, north_edge, pltpu.roll(v, 127, 1))
            south = jnp.where(lane == 0, south_edge, pltpu.roll(v, 1, 1))
            above = jnp.concatenate([v[16:], v[112:]], axis=0)
            below = jnp.concatenate([v[:16], v[:112]], axis=0)
            laplace = (
                east.reshape(128, 128)
                + west.reshape(128, 128)
                + north
                + south
                + above
                + below
                - 6.0 * v
            )
            store(j, (v + jnp.concatenate([rate] * 8, axis=0) * laplace).reshape(8, 16, 128))

    def store_field(j, value):
        field[1, j] = value

    def store_out(j, value):
        diffused_out[j] = value

    def deposit(tile):
        cells = cells_in[tile]
        rounded = arrived[tile].astype(bf16)
        low_hot = hot_rows(lax.bitwise_and(cells, LOW - 1), LOW)
        high = jnp.broadcast_to(lax.shift_right_arithmetic(cells, 8).astype(f32), (16, capacity))
        high = high.astype(bf16)
        zero = jnp.zeros_like(rounded)
        rows = lax.broadcasted_iota(jnp.int32, (16, capacity), 0).astype(f32).astype(bf16)
        spread = jnp.concatenate(
            [jnp.where(high == float(h), rounded, zero) for h in range(16)]
            + [jnp.where(high == rows, jnp.ones_like(zero), zero)],
            axis=0,
        )
        deposit_out[...] += lax.dot_general(
            spread, low_hot, (((1,), (1,)), ((), ())), preferred_element_type=f32
        )

    def keep(tile):
        pltpu.make_async_copy(arrived.at[tile], arrived_out.at[tile], out_sem.at[tile]).start()
        pltpu.make_async_copy(cells_in.at[tile], cells_out.at[tile], out_cell_sem.at[tile]).start()

    def kept(tile):
        pltpu.make_async_copy(arrived.at[tile], arrived_out.at[tile], out_sem.at[tile]).wait()
        pltpu.make_async_copy(cells_in.at[tile], cells_out.at[tile], out_cell_sem.at[tile]).wait()

    def receive(step, carry):
        from_lon, from_lat, tile = partner(step, -1)
        pltpu.make_async_remote_copy(
            src_ref=marked.at[tile],
            dst_ref=cells_in.at[tile],
            send_sem=send_cell_sem.at[tile],
            recv_sem=recv_cell_sem.at[tile],
            device_id=(from_lon, from_lat),
            device_id_type=MESH,
        ).wait_recv()
        pltpu.make_async_remote_copy(
            src_ref=species_hbm.at[tile],
            dst_ref=arrived.at[tile],
            send_sem=send_sem.at[tile],
            recv_sem=recv_sem.at[tile],
            device_id=(from_lon, from_lat),
            device_id_type=MESH,
        ).wait_recv()
        keep(tile)
        deposit(tile)
        return carry

    def settle(step):
        to_lon, to_lat, tile = partner(step, 1)
        cells_copy(to_lon, to_lat, tile).wait_send()
        species_copy(to_lon, to_lat, tile).wait_send()
        _, _, tile = partner(step, -1)
        kept(tile)

    def settle_step(step, carry):
        settle(step)
        return carry

    def receive_send(step, carry):
        receive(step, carry)

        @pl.when(step + WINDOW < devices)
        def refill():
            send(step + WINDOW)

        @pl.when(step > LAG)
        def earlier():
            settle(step - LAG)

        return carry

    halo_start(0)

    spot = lax.broadcasted_iota(jnp.int32, (256, 16), 0)
    spots = lax.broadcasted_iota(jnp.int32, (256, 16), 1)
    tall = jnp.where(lax.rem(spot, 16) == spots, 1.0, 0.0).astype(bf16)
    prod = prod_ref[...]
    prod_hi = prod.astype(bf16)
    prod_lo = (prod - prod_hi.astype(f32)).astype(bf16)
    row = lax.broadcasted_iota(jnp.int32, (256, 256), 0)
    col = lax.broadcasted_iota(jnp.int32, (256, 256), 1)
    same = lax.rem(row // 16, 8) == lax.rem(col // 16, 8)
    wide = []
    for part in (prod_hi, prod_lo):
        half = jnp.dot(tall, part, preferred_element_type=f32).astype(bf16)
        wide.append(
            lax.dot_general(half, tall, (((1,), (1,)), ((), ())), preferred_element_type=f32)
        )
    weight_out[...] = jnp.where(
        same, jnp.where(row < 128, wide[0], jnp.where(col < 128, wide[1], 0.0)), 0.0
    ).astype(bf16)
    rates_out[0] = jnp.concatenate([1.0 + column(loss_ref[...], 128)] * 8, axis=0)
    rates_out[1] = jnp.concatenate([column(self_ref[...], 128)] * 8, axis=0)

    deposit_out[...] = jnp.zeros_like(deposit_out)
    cells_in[me] = marked[me]
    own.wait()
    keep(me)
    deposit(me)

    first = devices // 4
    second = devices // 2
    lax.fori_loop(1, first, receive_send, 0)
    diffuse(0, store_field)
    halo_start(1)
    lax.fori_loop(first, second, receive_send, 0)
    diffuse(1, store_out)
    lax.fori_loop(second, devices, receive_send, 0)

    lax.fori_loop(devices - LAG, devices, settle_step, 0)
    kept(me)


def react_kernel(
    arrived_hbm,
    cells_hbm,
    diffused_hbm,
    deposit_hbm,
    weight_hbm,
    rates_hbm,
    parcels_hbm,
    mixed_hbm,
    arrived_ref,
    cells_ref,
    diffused_ref,
    deposit_ref,
    weight_ref,
    rates_ref,
    mixed_ref,
    coarse,
    blended,
    load_sem,
    block_sem,
    out_sem,
    mixed_sem,
):
    devices, _, capacity = arrived_ref.shape
    chunk = min(capacity, CHUNK)
    parts = capacity // chunk
    groups = devices // 16 * parts

    loads = [
        pltpu.make_async_copy(source, target, load_sem.at[k])
        for k, (source, target) in enumerate(
            (
                (deposit_hbm, deposit_ref),
                (diffused_hbm, diffused_ref),
                (cells_hbm, cells_ref),
                (weight_hbm, weight_ref),
                (rates_hbm, rates_ref),
            )
        )
    ]
    for load in loads:
        load.start()

    def place(group):
        first = 16 * (group // parts)
        lanes = pl.ds(pl.multiple_of(lax.rem(group, parts) * chunk, 128), chunk)
        return first, lanes

    def block_copy(group):
        first, lanes = place(group)
        block = (pl.ds(first, 16), slice(None), lanes)
        return pltpu.make_async_copy(
            arrived_hbm.at[block], arrived_ref.at[block], block_sem.at[group]
        )

    def out_copy(group):
        first, lanes = place(group)
        block = (pl.ds(first, 16), slice(None), lanes)
        return pltpu.make_async_copy(
            arrived_ref.at[block], parcels_hbm.at[block], out_sem.at[group]
        )

    def block_start(group, carry):
        block_copy(group).start()
        return carry

    lax.fori_loop(0, groups, block_start, 0)
    loads[0].wait()
    loads[1].wait()

    for h in range(16):
        for side in range(2):
            lanes = slice(128 * side, 128 * (side + 1))
            j = 2 * (h % 2) + side
            number = deposit_ref[256 + h : 257 + h, lanes]
            value = (
                diffused_ref[j, h // 2] + grid_weight * deposit_ref[16 * h : 16 * (h + 1), lanes]
            ) / (1.0 + grid_weight * number)
            mixed_ref[:, h // 2, j, :] = value
            coarse[16 * h : 16 * (h + 1), lanes] = value.astype(bf16)
    mixed_copy = pltpu.make_async_copy(mixed_ref, mixed_hbm, mixed_sem)
    mixed_copy.start()
    for load in loads[2:]:
        load.wait()

    loss = jnp.concatenate([rates_ref[0]] * (chunk // 128), axis=1)
    self_loss = jnp.concatenate([rates_ref[1]] * (chunk // 128), axis=1)

    def blend(group, source):
        first, lanes = place(group)
        cells = cells_ref[first + source, :, lanes]
        low_hot = hot_rows(lax.bitwise_and(cells, LOW - 1), LOW)
        picked = jnp.dot(coarse[...], low_hot, preferred_element_type=f32)
        high = jnp.broadcast_to(lax.shift_right_arithmetic(cells, 8), (8, chunk))
        upper, lower = picked[:8], picked[8:16]
        for h in range(1, 16):
            here = high == h
            upper = jnp.where(here, picked[16 * h : 16 * h + 8], upper)
            lower = jnp.where(here, picked[16 * h + 8 : 16 * h + 16], lower)
        found = jnp.concatenate([upper, lower], axis=0)
        start = arrived_ref[first + source, :, lanes]
        blended[group, 16 * source : 16 * (source + 1), :] = start + parcel_pull * (found - start)

    def sweep(group, states):
        later = []
        for k, state in enumerate(states):
            high_part = state.astype(bf16)
            low_part = (state - high_part.astype(f32)).astype(bf16)
            product = jnp.dot(
                weight_ref[...],
                jnp.concatenate([high_part, low_part], axis=0),
                preferred_element_type=f32,
            )
            produced = blended[group, 128 * k : 128 * (k + 1), :] + (
                product[:128] + product[128:]
            )
            bottom = loss + self_loss * state
            inverse = pl.reciprocal(bottom, approx=True)
            later.append(produced * (inverse * (2.0 - bottom * inverse)))
        return later

    def begin(group):
        return [blended[group, 128 * k : 128 * (k + 1), :] for k in range(2)]

    def finish(group, states):
        first, lanes = place(group)
        for k in range(16):
            alive = jnp.broadcast_to(cells_ref[first + k, :, lanes] >= 0, (16, chunk))
            arrived_ref[first + k, :, lanes] = jnp.where(
                alive, states[k // 8][16 * (k % 8) : 16 * (k % 8 + 1)], 0.0
            )
        out_copy(group).start()

    block_copy(0).wait()
    for source in range(16):
        blend(0, source)

    def both(group, carry):
        block_copy(group).wait()
        states = begin(group - 1)
        for source in range(16):
            blend(group, source)
            if source % 4 == 3:
                states = sweep(group - 1, states)
        finish(group - 1, states)
        return carry

    lax.fori_loop(1, groups, both, 0)
    states = begin(groups - 1)
    for _ in range(ITERS):
        states = sweep(groups - 1, states)
    finish(groups - 1, states)

    def out_wait(group, carry):
        out_copy(group).wait()
        return carry

    lax.fori_loop(0, groups, out_wait, 0)
    mixed_copy.wait()


def local(
    send_species, send_cells, send_counts, grid_state, diff_rate, prod_rate, loss_rate, self_rate
):
    n_lon = lax.axis_size("lon")
    n_lat = lax.axis_size("lat")
    devices, species_count, capacity = send_species.shape
    vmem = pl.BlockSpec(memory_space=pltpu.VMEM)
    hbm = pl.BlockSpec(memory_space=pl.ANY)
    arrived, cells, diffused, deposit, weight, rates = pl.pallas_call(
        functools.partial(exchange_kernel, n_lon, n_lat),
        out_shape=(
            jax.ShapeDtypeStruct((devices, species_count, capacity), f32),
            jax.ShapeDtypeStruct((devices, 1, capacity), jnp.int32),
            jax.ShapeDtypeStruct((4, 8, 16, 128), f32),
            jax.ShapeDtypeStruct((272, LOW), f32),
            jax.ShapeDtypeStruct((256, 256), bf16),
            jax.ShapeDtypeStruct((2, 128, 128), f32),
        ),
        in_specs=[pl.BlockSpec(memory_space=pltpu.HBM)] * 8,
        out_specs=(hbm, hbm, vmem, vmem, vmem, vmem),
        scratch_shapes=[
            pltpu.VMEM(send_cells.shape, jnp.int32),
            pltpu.SMEM(send_counts.shape, jnp.int32),
            pltpu.VMEM(grid_state.shape, f32),
            pltpu.VMEM((1, 16), f32),
            pltpu.VMEM((16, 16), f32),
            pltpu.VMEM((1, 16), f32),
            pltpu.VMEM((1, 16), f32),
            pltpu.SemaphoreType.DMA((7,)),
            pltpu.VMEM((devices, species_count, capacity), f32),
            pltpu.VMEM((devices, 1, capacity), jnp.int32),
            pltpu.VMEM((devices, 1, capacity), jnp.int32),
            pltpu.VMEM((2, 4, 8, 16, 128), f32),
            pltpu.VMEM((2, 8, 16, 128), f32),
            pltpu.VMEM((2, 8, 16, 128), f32),
            pltpu.VMEM((2, 8, 128), f32),
            pltpu.VMEM((2, 8, 128), f32),
            pltpu.VMEM((2, 2, 8, 128), f32),
            pltpu.SemaphoreType.DMA((devices,)),
            pltpu.SemaphoreType.DMA((devices,)),
            pltpu.SemaphoreType.DMA((devices,)),
            pltpu.SemaphoreType.DMA((devices,)),
            pltpu.SemaphoreType.DMA((devices,)),
            pltpu.SemaphoreType.DMA((devices,)),
            pltpu.SemaphoreType.DMA((2, 4)),
            pltpu.SemaphoreType.DMA((2, 4)),
        ],
        compiler_params=pltpu.CompilerParams(
            collective_id=0, has_side_effects=True, vmem_limit_bytes=VMEM_BYTES
        ),
        name="exchange",
    )(
        send_species,
        send_cells,
        send_counts,
        grid_state,
        diff_rate.reshape(1, 16),
        prod_rate,
        loss_rate.reshape(1, 16),
        self_rate.reshape(1, 16),
    )

    chunk = min(capacity, CHUNK)
    groups = devices // 16 * (capacity // chunk)
    return pl.pallas_call(
        react_kernel,
        out_shape=(
            jax.ShapeDtypeStruct(send_species.shape, f32),
            jax.ShapeDtypeStruct(grid_state.shape, f32),
        ),
        in_specs=[hbm] * 6,
        out_specs=(hbm, hbm),
        scratch_shapes=[
            pltpu.VMEM(send_species.shape, f32),
            pltpu.VMEM((devices, 1, capacity), jnp.int32),
            pltpu.VMEM((4, 8, 16, 128), f32),
            pltpu.VMEM((272, LOW), f32),
            pltpu.VMEM((256, 256), bf16),
            pltpu.VMEM((2, 128, 128), f32),
            pltpu.VMEM(grid_state.shape, f32),
            pltpu.VMEM((256, LOW), bf16),
            pltpu.VMEM((groups, 256, chunk), f32),
            pltpu.SemaphoreType.DMA((5,)),
            pltpu.SemaphoreType.DMA((groups,)),
            pltpu.SemaphoreType.DMA((groups,)),
            pltpu.SemaphoreType.DMA,
        ],
        compiler_params=pltpu.CompilerParams(vmem_limit_bytes=VMEM_BYTES),
        name="react",
    )(arrived, cells, diffused, deposit, weight, rates)


def solution(mesh):
    placed = (
        P(("lon", "lat"), None, None),
        P(("lon", "lat"), None),
        P(("lon", "lat")),
        P(None, None, "lon", "lat"),
        P(),
        P(),
        P(),
        P(),
    )
    return jax.shard_map(
        local,
        mesh=mesh,
        in_specs=placed,
        out_specs=(P(("lon", "lat"), None, None), P(None, None, "lon", "lat")),
        check_vma=False,
    )
```

```python
import functools

import jax
import jax.numpy as jnp
from jax import lax
from jax.experimental import pallas as pl
from jax.experimental.pallas import tpu as pltpu
from jax.sharding import PartitionSpec as P

ITERS = 4
LOW = 256
WINDOW = 4
LAG = 2
CHUNK = 256
VMEM_BYTES = 62 * 1024 * 1024

grid_weight = 0.5
parcel_pull = 0.3

f32 = jnp.float32
bf16 = jnp.bfloat16
MESH = pl.DeviceIdType.MESH


def hot_rows(index_row, count):
    wide = jnp.broadcast_to(index_row.astype(f32), (16, index_row.shape[1])).astype(bf16)
    rows = lax.broadcasted_iota(jnp.int32, (16, index_row.shape[1]), 0).astype(f32).astype(bf16)
    one = jnp.ones_like(wide)
    zero = jnp.zeros_like(wide)
    return jnp.concatenate(
        [jnp.where(wide == rows + float(16 * g), one, zero) for g in range(count // 16)], axis=0
    )


def exchange_kernel(
    n_lon,
    n_lat,
    species_hbm,
    cells_hbm,
    counts_hbm,
    grid_hbm,
    rate_hbm,
    prod_hbm,
    loss_hbm,
    self_hbm,
    arrived_out,
    cells_out,
    diffused_hbm,
    deposit_hbm,
    weight_hbm,
    rates_hbm,
    diffused_out,
    deposit_out,
    weight_out,
    rates_out,
    result_sem,
    cells_ref,
    counts_ref,
    grid_ref,
    rate_ref,
    prod_ref,
    loss_ref,
    self_ref,
    load_sem,
    arrived,
    marked,
    cells_in,
    field,
    east_halo,
    west_halo,
    north_halo,
    south_halo,
    edges,
    send_sem,
    recv_sem,
    send_cell_sem,
    recv_cell_sem,
    out_sem,
    out_cell_sem,
    halo_send,
    halo_recv,
):
    devices = n_lon * n_lat
    species_count = 16
    capacity = cells_ref.shape[1]
    lon = lax.axis_index("lon")
    lat = lax.axis_index("lat")
    me = lon * n_lat + lat

    def partner(step, sign):
        a = step // n_lat
        past = (a + n_lon - 1) // n_lon
        to_lon = lax.rem(lon + sign * a + n_lon, n_lon)
        source_lon = lon if sign > 0 else to_lon
        b = lax.rem(step + (n_lat // 2) * past * lax.rem(source_lon, 2), n_lat)
        to_lat = lax.rem(lat + sign * b + n_lat, n_lat)
        return to_lon, to_lat, to_lon * n_lat + to_lat

    loads = [
        pltpu.make_async_copy(source, target, load_sem.at[k])
        for k, (source, target) in enumerate(
            (
                (cells_hbm, cells_ref),
                (counts_hbm, counts_ref),
                (grid_hbm, grid_ref),
                (rate_hbm, rate_ref),
                (prod_hbm, prod_ref),
                (loss_hbm, loss_ref),
                (self_hbm, self_ref),
            )
        )
    ]
    for load in loads:
        load.start()
    results = [
        pltpu.make_async_copy(source, target, result_sem.at[k])
        for k, (source, target) in enumerate(
            (
                (weight_out, weight_hbm),
                (rates_out, rates_hbm),
                (diffused_out, diffused_hbm),
                (deposit_out, deposit_hbm),
            )
        )
    ]
    barrier = pltpu.get_barrier_semaphore()

    def greet(step, carry):
        to_lon, to_lat, _ = partner(step, 1)
        pl.semaphore_signal(barrier, inc=1, device_id=(to_lon, to_lat), device_id_type=MESH)
        return carry

    lax.fori_loop(1, devices, greet, 0)

    own = pltpu.make_async_copy(species_hbm.at[me], arrived.at[me], recv_sem.at[me])
    own.start()

    loads[0].wait()
    loads[1].wait()
    slot = lax.broadcasted_iota(jnp.int32, (1, capacity), 1)

    def mark(row, carry):
        marked[row] = jnp.where(slot < counts_ref[row], cells_ref[pl.ds(row, 1), :], -1)
        return carry

    lax.fori_loop(0, devices, mark, 0)
    pl.semaphore_wait(barrier, devices - 1)

    def species_copy(to_lon, to_lat, tile):
        return pltpu.make_async_remote_copy(
            src_ref=species_hbm.at[tile],
            dst_ref=arrived.at[me],
            send_sem=send_sem.at[tile],
            recv_sem=recv_sem.at[me],
            device_id=(to_lon, to_lat),
            device_id_type=MESH,
        )

    def cells_copy(to_lon, to_lat, tile):
        return pltpu.make_async_remote_copy(
            src_ref=marked.at[tile],
            dst_ref=cells_in.at[me],
            send_sem=send_cell_sem.at[tile],
            recv_sem=recv_cell_sem.at[me],
            device_id=(to_lon, to_lat),
            device_id_type=MESH,
        )

    def send(step):
        to_lon, to_lat, tile = partner(step, 1)
        cells_copy(to_lon, to_lat, tile).start()
        species_copy(to_lon, to_lat, tile).start()

    def send_step(step, carry):
        send(step)
        return carry

    lax.fori_loop(1, WINDOW + 1, send_step, 0)
    for load in loads[2:]:
        load.wait()

    for j in range(4):
        for level in range(8):
            field[0, j, level] = grid_ref[:, level, j, :]

    def halo_copies(turn):
        up_lon = lax.rem(lon + 1, n_lon)
        down_lon = lax.rem(lon + n_lon - 1, n_lon)
        up_lat = lax.rem(lat + 1, n_lat)
        down_lat = lax.rem(lat + n_lat - 1, n_lat)
        plan = (
            (field.at[turn, 0], east_halo.at[turn], (down_lon, lat)),
            (field.at[turn, 3], west_halo.at[turn], (up_lon, lat)),
            (edges.at[turn, 0], north_halo.at[turn], (lon, down_lat)),
            (edges.at[turn, 1], south_halo.at[turn], (lon, up_lat)),
        )
        return [
            pltpu.make_async_remote_copy(
                src_ref=source,
                dst_ref=target,
                send_sem=halo_send.at[turn, k],
                recv_sem=halo_recv.at[turn, k],
                device_id=device,
                device_id_type=MESH,
            )
            for k, (source, target, device) in enumerate(plan)
        ]

    def halo_start(turn):
        edges[turn] = jnp.zeros_like(edges[turn])
        for j in range(4):
            turned = field[turn, j].reshape(128, 128).T
            edges[turn, 0, j : j + 1, :] = turned[0:1, :]
            edges[turn, 1, j : j + 1, :] = turned[127:128, :]
        for copy in halo_copies(turn):
            copy.start()

    def column(row, lane_count):
        pick = lax.broadcasted_iota(jnp.int32, (16, 16), 0) == lax.broadcasted_iota(
            jnp.int32, (16, 16), 1
        )
        return jnp.broadcast_to(
            jnp.sum(jnp.where(pick, row, 0.0), axis=1, keepdims=True), (16, lane_count)
        )

    rate = column(rate_ref[...], 128)
    lane = lax.broadcasted_iota(jnp.int32, (128, 128), 1)

    def diffuse(turn, store):
        for copy in halo_copies(turn):
            copy.wait()
        north_cols = north_halo[turn].T
        south_cols = south_halo[turn].T
        for j in range(4):
            v = field[turn, j].reshape(128, 128)
            east = east_halo[turn] if j == 3 else field[turn, j + 1]
            west = west_halo[turn] if j == 0 else field[turn, j - 1]
            north_col = jnp.broadcast_to(north_cols[:, j : j + 1], (128, 128))
            south_col = jnp.broadcast_to(south_cols[:, j : j + 1], (128, 128))
            north_edge = jnp.where(lat == n_lat - 1, v, north_col)
            south_edge = jnp.where(lat == 0, v, south_col)
            north = jnp.where(lane == 127, north_edge, pltpu.roll(v, 127, 1))
            south = jnp.where(lane == 0, south_edge, pltpu.roll(v, 1, 1))
            above = jnp.concatenate([v[16:], v[112:]], axis=0)
            below = jnp.concatenate([v[:16], v[:112]], axis=0)
            laplace = (
                east.reshape(128, 128)
                + west.reshape(128, 128)
                + north
                + south
                + above
                + below
                - 6.0 * v
            )
            store(j, (v + jnp.concatenate([rate] * 8, axis=0) * laplace).reshape(8, 16, 128))

    def store_field(j, value):
        field[1, j] = value

    def store_out(j, value):
        diffused_out[j] = value

    def deposit(tile):
        cells = cells_in[tile]
        rounded = arrived[tile].astype(bf16)
        low_hot = hot_rows(lax.bitwise_and(cells, LOW - 1), LOW)
        high = jnp.broadcast_to(lax.shift_right_arithmetic(cells, 8).astype(f32), (16, capacity))
        high = high.astype(bf16)
        zero = jnp.zeros_like(rounded)
        rows = lax.broadcasted_iota(jnp.int32, (16, capacity), 0).astype(f32).astype(bf16)
        spread = jnp.concatenate(
            [jnp.where(high == float(h), rounded, zero) for h in range(16)]
            + [jnp.where(high == rows, jnp.ones_like(zero), zero)],
            axis=0,
        )
        deposit_out[...] += lax.dot_general(
            spread, low_hot, (((1,), (1,)), ((), ())), preferred_element_type=f32
        )

    def keep(tile):
        pltpu.make_async_copy(arrived.at[tile], arrived_out.at[tile], out_sem.at[tile]).start()
        pltpu.make_async_copy(cells_in.at[tile], cells_out.at[tile], out_cell_sem.at[tile]).start()

    def kept(tile):
        pltpu.make_async_copy(arrived.at[tile], arrived_out.at[tile], out_sem.at[tile]).wait()
        pltpu.make_async_copy(cells_in.at[tile], cells_out.at[tile], out_cell_sem.at[tile]).wait()

    def receive(step, carry):
        from_lon, from_lat, tile = partner(step, -1)
        pltpu.make_async_remote_copy(
            src_ref=marked.at[tile],
            dst_ref=cells_in.at[tile],
            send_sem=send_cell_sem.at[tile],
            recv_sem=recv_cell_sem.at[tile],
            device_id=(from_lon, from_lat),
            device_id_type=MESH,
        ).wait_recv()
        pltpu.make_async_remote_copy(
            src_ref=species_hbm.at[tile],
            dst_ref=arrived.at[tile],
            send_sem=send_sem.at[tile],
            recv_sem=recv_sem.at[tile],
            device_id=(from_lon, from_lat),
            device_id_type=MESH,
        ).wait_recv()
        keep(tile)
        deposit(tile)
        return carry

    def settle(step):
        to_lon, to_lat, tile = partner(step, 1)
        cells_copy(to_lon, to_lat, tile).wait_send()
        species_copy(to_lon, to_lat, tile).wait_send()
        _, _, tile = partner(step, -1)
        kept(tile)

    def settle_step(step, carry):
        settle(step)
        return carry

    def receive_send(step, carry):
        receive(step, carry)

        @pl.when(step + WINDOW < devices)
        def refill():
            send(step + WINDOW)

        @pl.when(step > LAG)
        def earlier():
            settle(step - LAG)

        return carry

    halo_start(0)

    spot = lax.broadcasted_iota(jnp.int32, (256, 16), 0)
    spots = lax.broadcasted_iota(jnp.int32, (256, 16), 1)
    tall = jnp.where(lax.rem(spot, 16) == spots, 1.0, 0.0).astype(bf16)
    prod = prod_ref[...]
    prod_hi = prod.astype(bf16)
    prod_lo = (prod - prod_hi.astype(f32)).astype(bf16)
    row = lax.broadcasted_iota(jnp.int32, (256, 256), 0)
    col = lax.broadcasted_iota(jnp.int32, (256, 256), 1)
    same = lax.rem(row // 16, 8) == lax.rem(col // 16, 8)
    wide = []
    for part in (prod_hi, prod_lo):
        half = jnp.dot(tall, part, preferred_element_type=f32).astype(bf16)
        wide.append(
            lax.dot_general(half, tall, (((1,), (1,)), ((), ())), preferred_element_type=f32)
        )
    weight_out[...] = jnp.where(
        same, jnp.where(row < 128, wide[0], jnp.where(col < 128, wide[1], 0.0)), 0.0
    ).astype(bf16)
    rates_out[0] = jnp.concatenate([1.0 + column(loss_ref[...], 128)] * 8, axis=0)
    rates_out[1] = jnp.concatenate([column(self_ref[...], 128)] * 8, axis=0)

    results[0].start()
    results[1].start()

    deposit_out[...] = jnp.zeros_like(deposit_out)
    cells_in[me] = marked[me]
    own.wait()
    keep(me)
    deposit(me)

    first = devices // 4
    second = devices // 2
    lax.fori_loop(1, first, receive_send, 0)
    diffuse(0, store_field)
    halo_start(1)
    lax.fori_loop(first, second, receive_send, 0)
    diffuse(1, store_out)
    results[2].start()
    lax.fori_loop(second, devices, receive_send, 0)

    results[3].start()
    lax.fori_loop(devices - LAG, devices, settle_step, 0)
    kept(me)
    for result in results:
        result.wait()


def react_kernel(
    arrived_hbm,
    cells_hbm,
    diffused_hbm,
    deposit_hbm,
    weight_hbm,
    rates_hbm,
    parcels_hbm,
    mixed_hbm,
    arrived_ref,
    cells_ref,
    diffused_ref,
    deposit_ref,
    weight_ref,
    rates_ref,
    mixed_ref,
    coarse,
    blended,
    load_sem,
    block_sem,
    out_sem,
    mixed_sem,
):
    devices, _, capacity = arrived_ref.shape
    chunk = min(capacity, CHUNK)
    parts = capacity // chunk
    groups = devices // 16 * parts

    loads = [
        pltpu.make_async_copy(source, target, load_sem.at[k])
        for k, (source, target) in enumerate(
            (
                (deposit_hbm, deposit_ref),
                (diffused_hbm, diffused_ref),
                (cells_hbm, cells_ref),
                (weight_hbm, weight_ref),
                (rates_hbm, rates_ref),
            )
        )
    ]
    for load in loads:
        load.start()

    def place(group):
        first = 16 * (group // parts)
        lanes = pl.ds(pl.multiple_of(lax.rem(group, parts) * chunk, 128), chunk)
        return first, lanes

    def block_copy(group):
        first, lanes = place(group)
        block = (pl.ds(first, 16), slice(None), lanes)
        return pltpu.make_async_copy(
            arrived_hbm.at[block], arrived_ref.at[block], block_sem.at[group]
        )

    def out_copy(group):
        first, lanes = place(group)
        block = (pl.ds(first, 16), slice(None), lanes)
        return pltpu.make_async_copy(
            arrived_ref.at[block], parcels_hbm.at[block], out_sem.at[group]
        )

    def block_start(group, carry):
        block_copy(group).start()
        return carry

    lax.fori_loop(0, groups, block_start, 0)
    loads[0].wait()
    loads[1].wait()

    for h in range(16):
        for side in range(2):
            lanes = slice(128 * side, 128 * (side + 1))
            j = 2 * (h % 2) + side
            number = deposit_ref[256 + h : 257 + h, lanes]
            value = (
                diffused_ref[j, h // 2] + grid_weight * deposit_ref[16 * h : 16 * (h + 1), lanes]
            ) / (1.0 + grid_weight * number)
            mixed_ref[:, h // 2, j, :] = value
            coarse[16 * h : 16 * (h + 1), lanes] = value.astype(bf16)
    mixed_copy = pltpu.make_async_copy(mixed_ref, mixed_hbm, mixed_sem)
    mixed_copy.start()
    for load in loads[2:]:
        load.wait()

    loss = jnp.concatenate([rates_ref[0]] * (chunk // 128), axis=1)
    self_loss = jnp.concatenate([rates_ref[1]] * (chunk // 128), axis=1)

    def blend(group, source):
        first, lanes = place(group)
        cells = cells_ref[first + source, :, lanes]
        low_hot = hot_rows(lax.bitwise_and(cells, LOW - 1), LOW)
        picked = jnp.dot(coarse[...], low_hot, preferred_element_type=f32)
        high = jnp.broadcast_to(lax.shift_right_arithmetic(cells, 8), (8, chunk))
        upper, lower = picked[:8], picked[8:16]
        for h in range(1, 16):
            here = high == h
            upper = jnp.where(here, picked[16 * h : 16 * h + 8], upper)
            lower = jnp.where(here, picked[16 * h + 8 : 16 * h + 16], lower)
        found = jnp.concatenate([upper, lower], axis=0)
        start = arrived_ref[first + source, :, lanes]
        blended[group, 16 * source : 16 * (source + 1), :] = start + parcel_pull * (found - start)

    def sweep(group, states):
        later = []
        for k, state in enumerate(states):
            high_part = state.astype(bf16)
            low_part = (state - high_part.astype(f32)).astype(bf16)
            product = jnp.dot(
                weight_ref[...],
                jnp.concatenate([high_part, low_part], axis=0),
                preferred_element_type=f32,
            )
            produced = blended[group, 128 * k : 128 * (k + 1), :] + (
                product[:128] + product[128:]
            )
            bottom = loss + self_loss * state
            inverse = pl.reciprocal(bottom, approx=True)
            later.append(produced * (inverse * (2.0 - bottom * inverse)))
        return later

    def begin(group):
        return [blended[group, 128 * k : 128 * (k + 1), :] for k in range(2)]

    def finish(group, states):
        first, lanes = place(group)
        for k in range(16):
            alive = jnp.broadcast_to(cells_ref[first + k, :, lanes] >= 0, (16, chunk))
            arrived_ref[first + k, :, lanes] = jnp.where(
                alive, states[k // 8][16 * (k % 8) : 16 * (k % 8 + 1)], 0.0
            )
        out_copy(group).start()

    block_copy(0).wait()
    for source in range(16):
        blend(0, source)

    def both(group, carry):
        block_copy(group).wait()
        states = begin(group - 1)
        for source in range(16):
            blend(group, source)
            if source % 4 == 3:
                states = sweep(group - 1, states)
        finish(group - 1, states)
        return carry

    lax.fori_loop(1, groups, both, 0)
    states = begin(groups - 1)
    for _ in range(ITERS):
        states = sweep(groups - 1, states)
    finish(groups - 1, states)

    def out_wait(group, carry):
        out_copy(group).wait()
        return carry

    lax.fori_loop(0, groups, out_wait, 0)
    mixed_copy.wait()


def local(
    send_species, send_cells, send_counts, grid_state, diff_rate, prod_rate, loss_rate, self_rate
):
    n_lon = lax.axis_size("lon")
    n_lat = lax.axis_size("lat")
    devices, species_count, capacity = send_species.shape
    hbm = pl.BlockSpec(memory_space=pl.ANY)
    arrived, cells, diffused, deposit, weight, rates = pl.pallas_call(
        functools.partial(exchange_kernel, n_lon, n_lat),
        out_shape=(
            jax.ShapeDtypeStruct((devices, species_count, capacity), f32),
            jax.ShapeDtypeStruct((devices, 1, capacity), jnp.int32),
            jax.ShapeDtypeStruct((4, 8, 16, 128), f32),
            jax.ShapeDtypeStruct((272, LOW), f32),
            jax.ShapeDtypeStruct((256, 256), bf16),
            jax.ShapeDtypeStruct((2, 128, 128), f32),
        ),
        in_specs=[pl.BlockSpec(memory_space=pltpu.HBM)] * 8,
        out_specs=(hbm,) * 6,
        scratch_shapes=[
            pltpu.VMEM((4, 8, 16, 128), f32),
            pltpu.VMEM((272, LOW), f32),
            pltpu.VMEM((256, 256), bf16),
            pltpu.VMEM((2, 128, 128), f32),
            pltpu.SemaphoreType.DMA((4,)),
            pltpu.VMEM(send_cells.shape, jnp.int32),
            pltpu.SMEM(send_counts.shape, jnp.int32),
            pltpu.VMEM(grid_state.shape, f32),
            pltpu.VMEM((1, 16), f32),
            pltpu.VMEM((16, 16), f32),
            pltpu.VMEM((1, 16), f32),
            pltpu.VMEM((1, 16), f32),
            pltpu.SemaphoreType.DMA((7,)),
            pltpu.VMEM((devices, species_count, capacity), f32),
            pltpu.VMEM((devices, 1, capacity), jnp.int32),
            pltpu.VMEM((devices, 1, capacity), jnp.int32),
            pltpu.VMEM((2, 4, 8, 16, 128), f32),
            pltpu.VMEM((2, 8, 16, 128), f32),
            pltpu.VMEM((2, 8, 16, 128), f32),
            pltpu.VMEM((2, 8, 128), f32),
            pltpu.VMEM((2, 8, 128), f32),
            pltpu.VMEM((2, 2, 8, 128), f32),
            pltpu.SemaphoreType.DMA((devices,)),
            pltpu.SemaphoreType.DMA((devices,)),
            pltpu.SemaphoreType.DMA((devices,)),
            pltpu.SemaphoreType.DMA((devices,)),
            pltpu.SemaphoreType.DMA((devices,)),
            pltpu.SemaphoreType.DMA((devices,)),
            pltpu.SemaphoreType.DMA((2, 4)),
            pltpu.SemaphoreType.DMA((2, 4)),
        ],
        compiler_params=pltpu.CompilerParams(
            collective_id=0, has_side_effects=True, vmem_limit_bytes=VMEM_BYTES
        ),
        name="exchange",
    )(
        send_species,
        send_cells,
        send_counts,
        grid_state,
        diff_rate.reshape(1, 16),
        prod_rate,
        loss_rate.reshape(1, 16),
        self_rate.reshape(1, 16),
    )

    chunk = min(capacity, CHUNK)
    groups = devices // 16 * (capacity // chunk)
    return pl.pallas_call(
        react_kernel,
        out_shape=(
            jax.ShapeDtypeStruct(send_species.shape, f32),
            jax.ShapeDtypeStruct(grid_state.shape, f32),
        ),
        in_specs=[hbm] * 6,
        out_specs=(hbm, hbm),
        scratch_shapes=[
            pltpu.VMEM(send_species.shape, f32),
            pltpu.VMEM((devices, 1, capacity), jnp.int32),
            pltpu.VMEM((4, 8, 16, 128), f32),
            pltpu.VMEM((272, LOW), f32),
            pltpu.VMEM((256, 256), bf16),
            pltpu.VMEM((2, 128, 128), f32),
            pltpu.VMEM(grid_state.shape, f32),
            pltpu.VMEM((256, LOW), bf16),
            pltpu.VMEM((groups, 256, chunk), f32),
            pltpu.SemaphoreType.DMA((5,)),
            pltpu.SemaphoreType.DMA((groups,)),
            pltpu.SemaphoreType.DMA((groups,)),
            pltpu.SemaphoreType.DMA,
        ],
        compiler_params=pltpu.CompilerParams(vmem_limit_bytes=VMEM_BYTES),
        name="react",
    )(arrived, cells, diffused, deposit, weight, rates)


def solution(mesh):
    placed = (
        P(("lon", "lat"), None, None),
        P(("lon", "lat"), None),
        P(("lon", "lat")),
        P(None, None, "lon", "lat"),
        P(),
        P(),
        P(),
        P(),
    )
    return jax.shard_map(
        local,
        mesh=mesh,
        in_specs=placed,
        out_specs=(P(("lon", "lat"), None, None), P(None, None, "lon", "lat")),
        check_vma=False,
    )
```

```python
import functools

import jax
import jax.numpy as jnp
from jax import lax
from jax.experimental import pallas as pl
from jax.experimental.pallas import tpu as pltpu
from jax.sharding import PartitionSpec as P

ITERS = 4
LOW = 256
WINDOW = 12
LAG = 2
CHUNK = 256
VMEM_BYTES = 62 * 1024 * 1024

grid_weight = 0.5
parcel_pull = 0.3

f32 = jnp.float32
bf16 = jnp.bfloat16
MESH = pl.DeviceIdType.MESH


def hot_rows(index_row, count):
    wide = jnp.broadcast_to(index_row.astype(f32), (16, index_row.shape[1])).astype(bf16)
    rows = lax.broadcasted_iota(jnp.int32, (16, index_row.shape[1]), 0).astype(f32).astype(bf16)
    one = jnp.ones_like(wide)
    zero = jnp.zeros_like(wide)
    return jnp.concatenate(
        [jnp.where(wide == rows + float(16 * g), one, zero) for g in range(count // 16)], axis=0
    )


def exchange_kernel(
    n_lon,
    n_lat,
    species_hbm,
    cells_hbm,
    counts_hbm,
    grid_hbm,
    rate_hbm,
    prod_hbm,
    loss_hbm,
    self_hbm,
    arrived_out,
    cells_out,
    diffused_hbm,
    deposit_hbm,
    weight_hbm,
    rates_hbm,
    diffused_out,
    deposit_out,
    weight_out,
    rates_out,
    result_sem,
    cells_ref,
    counts_ref,
    grid_ref,
    rate_ref,
    prod_ref,
    loss_ref,
    self_ref,
    load_sem,
    arrived,
    marked,
    cells_in,
    field,
    east_halo,
    west_halo,
    north_halo,
    south_halo,
    edges,
    send_sem,
    recv_sem,
    send_cell_sem,
    recv_cell_sem,
    out_sem,
    out_cell_sem,
    halo_send,
    halo_recv,
):
    devices = n_lon * n_lat
    species_count = 16
    capacity = cells_ref.shape[1]
    lon = lax.axis_index("lon")
    lat = lax.axis_index("lat")
    me = lon * n_lat + lat

    def partner(step, sign):
        a = step // n_lat
        past = (a + n_lon - 1) // n_lon
        to_lon = lax.rem(lon + sign * a + n_lon, n_lon)
        source_lon = lon if sign > 0 else to_lon
        b = lax.rem(step + (n_lat // 2) * past * lax.rem(source_lon, 2), n_lat)
        to_lat = lax.rem(lat + sign * b + n_lat, n_lat)
        return to_lon, to_lat, to_lon * n_lat + to_lat

    barrier = pltpu.get_barrier_semaphore()

    def greet(step, carry):
        to_lon, to_lat, _ = partner(step, 1)
        pl.semaphore_signal(barrier, inc=1, device_id=(to_lon, to_lat), device_id_type=MESH)
        return carry

    lax.fori_loop(1, devices, greet, 0)

    loads = [
        pltpu.make_async_copy(source, target, load_sem.at[k])
        for k, (source, target) in enumerate(
            (
                (cells_hbm, cells_ref),
                (counts_hbm, counts_ref),
                (grid_hbm, grid_ref),
                (rate_hbm, rate_ref),
                (prod_hbm, prod_ref),
                (loss_hbm, loss_ref),
                (self_hbm, self_ref),
            )
        )
    ]
    for load in loads:
        load.start()
    results = [
        pltpu.make_async_copy(source, target, result_sem.at[k])
        for k, (source, target) in enumerate(
            (
                (weight_out, weight_hbm),
                (rates_out, rates_hbm),
                (diffused_out, diffused_hbm),
                (deposit_out, deposit_hbm),
            )
        )
    ]
    own = pltpu.make_async_copy(species_hbm.at[me], arrived.at[me], recv_sem.at[me])
    own.start()

    loads[0].wait()
    loads[1].wait()
    slot = lax.broadcasted_iota(jnp.int32, (1, capacity), 1)

    def mark(row, carry):
        marked[row] = jnp.where(slot < counts_ref[row], cells_ref[pl.ds(row, 1), :], -1)
        return carry

    lax.fori_loop(0, devices, mark, 0)
    pl.semaphore_wait(barrier, devices - 1)

    def species_copy(to_lon, to_lat, tile):
        return pltpu.make_async_remote_copy(
            src_ref=species_hbm.at[tile],
            dst_ref=arrived.at[me],
            send_sem=send_sem.at[tile],
            recv_sem=recv_sem.at[me],
            device_id=(to_lon, to_lat),
            device_id_type=MESH,
        )

    def cells_copy(to_lon, to_lat, tile):
        return pltpu.make_async_remote_copy(
            src_ref=marked.at[tile],
            dst_ref=cells_in.at[me],
            send_sem=send_cell_sem.at[tile],
            recv_sem=recv_cell_sem.at[me],
            device_id=(to_lon, to_lat),
            device_id_type=MESH,
        )

    def send(step):
        to_lon, to_lat, tile = partner(step, 1)
        cells_copy(to_lon, to_lat, tile).start()
        species_copy(to_lon, to_lat, tile).start()

    def send_step(step, carry):
        send(step)
        return carry

    lax.fori_loop(1, WINDOW + 1, send_step, 0)
    for load in loads[2:]:
        load.wait()

    for j in range(4):
        for level in range(8):
            field[0, j, level] = grid_ref[:, level, j, :]

    def halo_copies(turn):
        up_lon = lax.rem(lon + 1, n_lon)
        down_lon = lax.rem(lon + n_lon - 1, n_lon)
        up_lat = lax.rem(lat + 1, n_lat)
        down_lat = lax.rem(lat + n_lat - 1, n_lat)
        plan = (
            (field.at[turn, 0], east_halo.at[turn], (down_lon, lat)),
            (field.at[turn, 3], west_halo.at[turn], (up_lon, lat)),
            (edges.at[turn, 0], north_halo.at[turn], (lon, down_lat)),
            (edges.at[turn, 1], south_halo.at[turn], (lon, up_lat)),
        )
        return [
            pltpu.make_async_remote_copy(
                src_ref=source,
                dst_ref=target,
                send_sem=halo_send.at[turn, k],
                recv_sem=halo_recv.at[turn, k],
                device_id=device,
                device_id_type=MESH,
            )
            for k, (source, target, device) in enumerate(plan)
        ]

    def halo_start(turn):
        edges[turn] = jnp.zeros_like(edges[turn])
        for j in range(4):
            turned = field[turn, j].reshape(128, 128).T
            edges[turn, 0, j : j + 1, :] = turned[0:1, :]
            edges[turn, 1, j : j + 1, :] = turned[127:128, :]
        for copy in halo_copies(turn):
            copy.start()

    def column(row, lane_count):
        pick = lax.broadcasted_iota(jnp.int32, (16, 16), 0) == lax.broadcasted_iota(
            jnp.int32, (16, 16), 1
        )
        return jnp.broadcast_to(
            jnp.sum(jnp.where(pick, row, 0.0), axis=1, keepdims=True), (16, lane_count)
        )

    rate = column(rate_ref[...], 128)
    lane = lax.broadcasted_iota(jnp.int32, (128, 128), 1)

    def diffuse(turn, store):
        for copy in halo_copies(turn):
            copy.wait()
        north_cols = north_halo[turn].T
        south_cols = south_halo[turn].T
        for j in range(4):
            v = field[turn, j].reshape(128, 128)
            east = east_halo[turn] if j == 3 else field[turn, j + 1]
            west = west_halo[turn] if j == 0 else field[turn, j - 1]
            north_col = jnp.broadcast_to(north_cols[:, j : j + 1], (128, 128))
            south_col = jnp.broadcast_to(south_cols[:, j : j + 1], (128, 128))
            north_edge = jnp.where(lat == n_lat - 1, v, north_col)
            south_edge = jnp.where(lat == 0, v, south_col)
            north = jnp.where(lane == 127, north_edge, pltpu.roll(v, 127, 1))
            south = jnp.where(lane == 0, south_edge, pltpu.roll(v, 1, 1))
            above = jnp.concatenate([v[16:], v[112:]], axis=0)
            below = jnp.concatenate([v[:16], v[:112]], axis=0)
            laplace = (
                east.reshape(128, 128)
                + west.reshape(128, 128)
                + north
                + south
                + above
                + below
                - 6.0 * v
            )
            store(j, (v + jnp.concatenate([rate] * 8, axis=0) * laplace).reshape(8, 16, 128))

    def store_field(j, value):
        field[1, j] = value

    def store_out(j, value):
        diffused_out[j] = value

    def tables(tile):
        cells = cells_in[tile]
        rounded = arrived[tile].astype(bf16)
        low_hot = hot_rows(lax.bitwise_and(cells, LOW - 1), LOW)
        high = jnp.broadcast_to(lax.shift_right_arithmetic(cells, 8).astype(f32), (16, capacity))
        high = high.astype(bf16)
        zero = jnp.zeros_like(rounded)
        rows = lax.broadcasted_iota(jnp.int32, (16, capacity), 0).astype(f32).astype(bf16)
        spread = jnp.concatenate(
            [jnp.where(high == float(h), rounded, zero) for h in range(16)]
            + [jnp.where(high == rows, jnp.ones_like(zero), zero)],
            axis=0,
        )
        return spread, low_hot

    def deposit(one, other):
        spread_one, hot_one = tables(one)
        spread_other, hot_other = tables(other)
        deposit_out[...] += lax.dot_general(
            jnp.concatenate([spread_one, spread_other], axis=1),
            jnp.concatenate([hot_one, hot_other], axis=1),
            (((1,), (1,)), ((), ())),
            preferred_element_type=f32,
        )

    def keep(tile):
        pltpu.make_async_copy(arrived.at[tile], arrived_out.at[tile], out_sem.at[tile]).start()
        pltpu.make_async_copy(cells_in.at[tile], cells_out.at[tile], out_cell_sem.at[tile]).start()

    def kept(tile):
        pltpu.make_async_copy(arrived.at[tile], arrived_out.at[tile], out_sem.at[tile]).wait()
        pltpu.make_async_copy(cells_in.at[tile], cells_out.at[tile], out_cell_sem.at[tile]).wait()

    def receive(step):
        from_lon, from_lat, tile = partner(step, -1)
        pltpu.make_async_remote_copy(
            src_ref=marked.at[tile],
            dst_ref=cells_in.at[tile],
            send_sem=send_cell_sem.at[tile],
            recv_sem=recv_cell_sem.at[tile],
            device_id=(from_lon, from_lat),
            device_id_type=MESH,
        ).wait_recv()
        pltpu.make_async_remote_copy(
            src_ref=species_hbm.at[tile],
            dst_ref=arrived.at[tile],
            send_sem=send_sem.at[tile],
            recv_sem=recv_sem.at[tile],
            device_id=(from_lon, from_lat),
            device_id_type=MESH,
        ).wait_recv()
        keep(tile)
        return tile

    def settle(step):
        to_lon, to_lat, tile = partner(step, 1)
        cells_copy(to_lon, to_lat, tile).wait_send()
        species_copy(to_lon, to_lat, tile).wait_send()
        _, _, tile = partner(step, -1)
        kept(tile)

    def settle_step(step, carry):
        settle(step)
        return carry

    def receive_send(pair, carry):
        tiles = []
        for step in (2 * pair, 2 * pair + 1):
            tiles.append(receive(step))

            @pl.when(step + WINDOW < devices)
            def refill():
                send(step + WINDOW)

        deposit(*tiles)
        for step in (2 * pair, 2 * pair + 1):

            @pl.when(step > LAG)
            def earlier():
                settle(step - LAG)

        return carry

    halo_start(0)

    spot = lax.broadcasted_iota(jnp.int32, (256, 16), 0)
    spots = lax.broadcasted_iota(jnp.int32, (256, 16), 1)
    tall = jnp.where(lax.rem(spot, 16) == spots, 1.0, 0.0).astype(bf16)
    prod = prod_ref[...]
    prod_hi = prod.astype(bf16)
    prod_lo = (prod - prod_hi.astype(f32)).astype(bf16)
    row = lax.broadcasted_iota(jnp.int32, (256, 256), 0)
    col = lax.broadcasted_iota(jnp.int32, (256, 256), 1)
    same = lax.rem(row // 16, 8) == lax.rem(col // 16, 8)
    wide = []
    for part in (prod_hi, prod_lo):
        half = jnp.dot(tall, part, preferred_element_type=f32).astype(bf16)
        wide.append(
            lax.dot_general(half, tall, (((1,), (1,)), ((), ())), preferred_element_type=f32)
        )
    weight_out[...] = jnp.where(
        same, jnp.where(row < 128, wide[0], jnp.where(col < 128, wide[1], 0.0)), 0.0
    ).astype(bf16)
    rates_out[0] = jnp.concatenate([1.0 + column(loss_ref[...], 128)] * 8, axis=0)
    rates_out[1] = jnp.concatenate([column(self_ref[...], 128)] * 8, axis=0)

    results[0].start()
    results[1].start()

    deposit_out[...] = jnp.zeros_like(deposit_out)
    cells_in[me] = marked[me]
    own.wait()
    keep(me)
    near = receive(1)
    send(1 + WINDOW)
    deposit(me, near)

    first = devices // 8
    second = devices // 4
    lax.fori_loop(1, first, receive_send, 0)
    diffuse(0, store_field)
    halo_start(1)
    lax.fori_loop(first, second, receive_send, 0)
    diffuse(1, store_out)
    results[2].start()
    lax.fori_loop(second, devices // 2, receive_send, 0)

    results[3].start()
    lax.fori_loop(devices - LAG, devices, settle_step, 0)
    kept(me)
    for result in results:
        result.wait()


def react_kernel(
    arrived_hbm,
    cells_hbm,
    diffused_hbm,
    deposit_hbm,
    weight_hbm,
    rates_hbm,
    parcels_hbm,
    mixed_hbm,
    arrived_ref,
    cells_ref,
    diffused_ref,
    deposit_ref,
    weight_ref,
    rates_ref,
    mixed_ref,
    coarse,
    blended,
    load_sem,
    block_sem,
    out_sem,
    mixed_sem,
):
    devices, _, capacity = arrived_ref.shape
    chunk = min(capacity, CHUNK)
    parts = capacity // chunk
    groups = devices // 16 * parts

    loads = [
        pltpu.make_async_copy(source, target, load_sem.at[k])
        for k, (source, target) in enumerate(
            (
                (deposit_hbm, deposit_ref),
                (diffused_hbm, diffused_ref),
                (cells_hbm, cells_ref),
                (weight_hbm, weight_ref),
                (rates_hbm, rates_ref),
            )
        )
    ]
    for load in loads:
        load.start()

    def place(group):
        first = 16 * (group // parts)
        lanes = pl.ds(pl.multiple_of(lax.rem(group, parts) * chunk, 128), chunk)
        return first, lanes

    def block_copy(group):
        first, lanes = place(group)
        block = (pl.ds(first, 16), slice(None), lanes)
        return pltpu.make_async_copy(
            arrived_hbm.at[block], arrived_ref.at[block], block_sem.at[group]
        )

    def out_copy(group):
        first, lanes = place(group)
        block = (pl.ds(first, 16), slice(None), lanes)
        return pltpu.make_async_copy(
            arrived_ref.at[block], parcels_hbm.at[block], out_sem.at[group]
        )

    def block_start(group, carry):
        block_copy(group).start()
        return carry

    lax.fori_loop(0, groups, block_start, 0)
    loads[0].wait()
    loads[1].wait()

    for h in range(16):
        for side in range(2):
            lanes = slice(128 * side, 128 * (side + 1))
            j = 2 * (h % 2) + side
            number = deposit_ref[256 + h : 257 + h, lanes]
            value = (
                diffused_ref[j, h // 2] + grid_weight * deposit_ref[16 * h : 16 * (h + 1), lanes]
            ) / (1.0 + grid_weight * number)
            mixed_ref[:, h // 2, j, :] = value
            coarse[16 * h : 16 * (h + 1), lanes] = value.astype(bf16)
    mixed_copy = pltpu.make_async_copy(mixed_ref, mixed_hbm, mixed_sem)
    mixed_copy.start()
    for load in loads[2:]:
        load.wait()

    loss = jnp.concatenate([rates_ref[0]] * (chunk // 128), axis=1)
    self_loss = jnp.concatenate([rates_ref[1]] * (chunk // 128), axis=1)

    def blend(group, source):
        first, lanes = place(group)
        cells = cells_ref[first + source, :, lanes]
        low_hot = hot_rows(lax.bitwise_and(cells, LOW - 1), LOW)
        picked = jnp.dot(coarse[...], low_hot, preferred_element_type=f32)
        high = jnp.broadcast_to(lax.shift_right_arithmetic(cells, 8), (8, chunk))
        upper, lower = picked[:8], picked[8:16]
        for h in range(1, 16):
            here = high == h
            upper = jnp.where(here, picked[16 * h : 16 * h + 8], upper)
            lower = jnp.where(here, picked[16 * h + 8 : 16 * h + 16], lower)
        found = jnp.concatenate([upper, lower], axis=0)
        start = arrived_ref[first + source, :, lanes]
        blended[group, 16 * source : 16 * (source + 1), :] = start + parcel_pull * (found - start)

    def sweep(group, states):
        later = []
        for k, state in enumerate(states):
            high_part = state.astype(bf16)
            low_part = (state - high_part.astype(f32)).astype(bf16)
            product = jnp.dot(
                weight_ref[...],
                jnp.concatenate([high_part, low_part], axis=0),
                preferred_element_type=f32,
            )
            produced = blended[group, 128 * k : 128 * (k + 1), :] + (
                product[:128] + product[128:]
            )
            bottom = loss + self_loss * state
            inverse = pl.reciprocal(bottom, approx=True)
            later.append(produced * (inverse * (2.0 - bottom * inverse)))
        return later

    def begin(group):
        return [blended[group, 128 * k : 128 * (k + 1), :] for k in range(2)]

    def finish(group, states):
        first, lanes = place(group)
        for k in range(16):
            alive = jnp.broadcast_to(cells_ref[first + k, :, lanes] >= 0, (16, chunk))
            arrived_ref[first + k, :, lanes] = jnp.where(
                alive, states[k // 8][16 * (k % 8) : 16 * (k % 8 + 1)], 0.0
            )
        out_copy(group).start()

    block_copy(0).wait()
    for source in range(16):
        blend(0, source)

    def both(group, carry):
        block_copy(group).wait()
        states = begin(group - 1)
        for source in range(16):
            blend(group, source)
            if source % 4 == 3:
                states = sweep(group - 1, states)
        finish(group - 1, states)
        return carry

    lax.fori_loop(1, groups, both, 0)
    states = begin(groups - 1)
    for _ in range(ITERS):
        states = sweep(groups - 1, states)
    finish(groups - 1, states)

    def out_wait(group, carry):
        out_copy(group).wait()
        return carry

    lax.fori_loop(0, groups, out_wait, 0)
    mixed_copy.wait()


def local(
    send_species, send_cells, send_counts, grid_state, diff_rate, prod_rate, loss_rate, self_rate
):
    n_lon = lax.axis_size("lon")
    n_lat = lax.axis_size("lat")
    devices, species_count, capacity = send_species.shape
    hbm = pl.BlockSpec(memory_space=pl.ANY)
    arrived, cells, diffused, deposit, weight, rates = pl.pallas_call(
        functools.partial(exchange_kernel, n_lon, n_lat),
        out_shape=(
            jax.ShapeDtypeStruct((devices, species_count, capacity), f32),
            jax.ShapeDtypeStruct((devices, 1, capacity), jnp.int32),
            jax.ShapeDtypeStruct((4, 8, 16, 128), f32),
            jax.ShapeDtypeStruct((272, LOW), f32),
            jax.ShapeDtypeStruct((256, 256), bf16),
            jax.ShapeDtypeStruct((2, 128, 128), f32),
        ),
        in_specs=[pl.BlockSpec(memory_space=pltpu.HBM)] * 8,
        out_specs=(hbm,) * 6,
        scratch_shapes=[
            pltpu.VMEM((4, 8, 16, 128), f32),
            pltpu.VMEM((272, LOW), f32),
            pltpu.VMEM((256, 256), bf16),
            pltpu.VMEM((2, 128, 128), f32),
            pltpu.SemaphoreType.DMA((4,)),
            pltpu.VMEM(send_cells.shape, jnp.int32),
            pltpu.SMEM(send_counts.shape, jnp.int32),
            pltpu.VMEM(grid_state.shape, f32),
            pltpu.VMEM((1, 16), f32),
            pltpu.VMEM((16, 16), f32),
            pltpu.VMEM((1, 16), f32),
            pltpu.VMEM((1, 16), f32),
            pltpu.SemaphoreType.DMA((7,)),
            pltpu.VMEM((devices, species_count, capacity), f32),
            pltpu.VMEM((devices, 1, capacity), jnp.int32),
            pltpu.VMEM((devices, 1, capacity), jnp.int32),
            pltpu.VMEM((2, 4, 8, 16, 128), f32),
            pltpu.VMEM((2, 8, 16, 128), f32),
            pltpu.VMEM((2, 8, 16, 128), f32),
            pltpu.VMEM((2, 8, 128), f32),
            pltpu.VMEM((2, 8, 128), f32),
            pltpu.VMEM((2, 2, 8, 128), f32),
            pltpu.SemaphoreType.DMA((devices,)),
            pltpu.SemaphoreType.DMA((devices,)),
            pltpu.SemaphoreType.DMA((devices,)),
            pltpu.SemaphoreType.DMA((devices,)),
            pltpu.SemaphoreType.DMA((devices,)),
            pltpu.SemaphoreType.DMA((devices,)),
            pltpu.SemaphoreType.DMA((2, 4)),
            pltpu.SemaphoreType.DMA((2, 4)),
        ],
        compiler_params=pltpu.CompilerParams(
            collective_id=0, has_side_effects=True, vmem_limit_bytes=VMEM_BYTES
        ),
        name="exchange",
    )(
        send_species,
        send_cells,
        send_counts,
        grid_state,
        diff_rate.reshape(1, 16),
        prod_rate,
        loss_rate.reshape(1, 16),
        self_rate.reshape(1, 16),
    )

    chunk = min(capacity, CHUNK)
    groups = devices // 16 * (capacity // chunk)
    return pl.pallas_call(
        react_kernel,
        out_shape=(
            jax.ShapeDtypeStruct(send_species.shape, f32),
            jax.ShapeDtypeStruct(grid_state.shape, f32),
        ),
        in_specs=[hbm] * 6,
        out_specs=(hbm, hbm),
        scratch_shapes=[
            pltpu.VMEM(send_species.shape, f32),
            pltpu.VMEM((devices, 1, capacity), jnp.int32),
            pltpu.VMEM((4, 8, 16, 128), f32),
            pltpu.VMEM((272, LOW), f32),
            pltpu.VMEM((256, 256), bf16),
            pltpu.VMEM((2, 128, 128), f32),
            pltpu.VMEM(grid_state.shape, f32),
            pltpu.VMEM((256, LOW), bf16),
            pltpu.VMEM((groups, 256, chunk), f32),
            pltpu.SemaphoreType.DMA((5,)),
            pltpu.SemaphoreType.DMA((groups,)),
            pltpu.SemaphoreType.DMA((groups,)),
            pltpu.SemaphoreType.DMA,
        ],
        compiler_params=pltpu.CompilerParams(vmem_limit_bytes=VMEM_BYTES),
        name="react",
    )(arrived, cells, diffused, deposit, weight, rates)


def solution(mesh):
    placed = (
        P(("lon", "lat"), None, None),
        P(("lon", "lat"), None),
        P(("lon", "lat")),
        P(None, None, "lon", "lat"),
        P(),
        P(),
        P(),
        P(),
    )
    return jax.shard_map(
        local,
        mesh=mesh,
        in_specs=placed,
        out_specs=(P(("lon", "lat"), None, None), P(None, None, "lon", "lat")),
        check_vma=False,
    )
```

```python
import functools

import jax
import jax.numpy as jnp
from jax import lax
from jax.experimental import pallas as pl
from jax.experimental.pallas import tpu as pltpu
from jax.sharding import PartitionSpec as P

ITERS = 4
LOW = 256
WINDOW = 16
LAG = 2
CHUNK = 256
VMEM_BYTES = 62 * 1024 * 1024

grid_weight = 0.5
parcel_pull = 0.3

f32 = jnp.float32
bf16 = jnp.bfloat16
MESH = pl.DeviceIdType.MESH


def hot_rows(index_row, count):
    wide = jnp.broadcast_to(index_row.astype(f32), (16, index_row.shape[1])).astype(bf16)
    rows = lax.broadcasted_iota(jnp.int32, (16, index_row.shape[1]), 0).astype(f32).astype(bf16)
    one = jnp.ones_like(wide)
    zero = jnp.zeros_like(wide)
    return jnp.concatenate(
        [jnp.where(wide == rows + float(16 * g), one, zero) for g in range(count // 16)], axis=0
    )


def exchange_kernel(
    n_lon,
    n_lat,
    species_hbm,
    cells_hbm,
    counts_hbm,
    grid_hbm,
    rate_hbm,
    prod_hbm,
    loss_hbm,
    self_hbm,
    arrived_out,
    cells_out,
    diffused_hbm,
    deposit_hbm,
    weight_hbm,
    rates_hbm,
    diffused_out,
    deposit_out,
    weight_out,
    rates_out,
    result_sem,
    cells_ref,
    counts_ref,
    grid_ref,
    rate_ref,
    prod_ref,
    loss_ref,
    self_ref,
    load_sem,
    arrived,
    marked,
    cells_in,
    field,
    east_halo,
    west_halo,
    north_halo,
    south_halo,
    edges,
    send_sem,
    recv_sem,
    send_cell_sem,
    recv_cell_sem,
    out_sem,
    out_cell_sem,
    halo_send,
    halo_recv,
):
    devices = n_lon * n_lat
    species_count = 16
    capacity = cells_ref.shape[1]
    lon = lax.axis_index("lon")
    lat = lax.axis_index("lat")
    me = lon * n_lat + lat

    def partner(step, sign):
        a = step // n_lat
        past = (a + n_lon - 1) // n_lon
        to_lon = lax.rem(lon + sign * a + n_lon, n_lon)
        source_lon = lon if sign > 0 else to_lon
        b = lax.rem(step + (n_lat // 2) * past * lax.rem(source_lon, 2), n_lat)
        to_lat = lax.rem(lat + sign * b + n_lat, n_lat)
        return to_lon, to_lat, to_lon * n_lat + to_lat

    barrier = pltpu.get_barrier_semaphore()

    def greet(step, carry):
        to_lon, to_lat, _ = partner(step, 1)
        pl.semaphore_signal(barrier, inc=1, device_id=(to_lon, to_lat), device_id_type=MESH)
        return carry

    lax.fori_loop(1, devices, greet, 0)

    loads = [
        pltpu.make_async_copy(source, target, load_sem.at[k])
        for k, (source, target) in enumerate(
            (
                (cells_hbm, cells_ref),
                (counts_hbm, counts_ref),
                (grid_hbm, grid_ref),
                (rate_hbm, rate_ref),
                (prod_hbm, prod_ref),
                (loss_hbm, loss_ref),
                (self_hbm, self_ref),
            )
        )
    ]
    for load in loads:
        load.start()
    results = [
        pltpu.make_async_copy(source, target, result_sem.at[k])
        for k, (source, target) in enumerate(
            (
                (weight_out, weight_hbm),
                (rates_out, rates_hbm),
                (diffused_out, diffused_hbm),
                (deposit_out, deposit_hbm),
            )
        )
    ]
    own = pltpu.make_async_copy(species_hbm.at[me], arrived.at[me], recv_sem.at[me])
    own.start()

    loads[0].wait()
    loads[1].wait()
    slot = lax.broadcasted_iota(jnp.int32, (1, capacity), 1)

    def mark(row, carry):
        marked[row] = jnp.where(slot < counts_ref[row], cells_ref[pl.ds(row, 1), :], -1)
        return carry

    lax.fori_loop(0, devices, mark, 0)
    pl.semaphore_wait(barrier, devices - 1)

    def species_copy(to_lon, to_lat, tile):
        return pltpu.make_async_remote_copy(
            src_ref=species_hbm.at[tile],
            dst_ref=arrived.at[me],
            send_sem=send_sem.at[tile],
            recv_sem=recv_sem.at[me],
            device_id=(to_lon, to_lat),
            device_id_type=MESH,
        )

    def cells_copy(to_lon, to_lat, tile):
        return pltpu.make_async_remote_copy(
            src_ref=marked.at[tile],
            dst_ref=cells_in.at[me],
            send_sem=send_cell_sem.at[tile],
            recv_sem=recv_cell_sem.at[me],
            device_id=(to_lon, to_lat),
            device_id_type=MESH,
        )

    def send(step):
        to_lon, to_lat, tile = partner(step, 1)
        cells_copy(to_lon, to_lat, tile).start()
        species_copy(to_lon, to_lat, tile).start()

    def send_step(step, carry):
        send(step)
        return carry

    lax.fori_loop(1, WINDOW + 1, send_step, 0)
    for load in loads[2:]:
        load.wait()

    for j in range(4):
        for level in range(8):
            field[0, j, level] = grid_ref[:, level, j, :]

    def halo_copies(turn):
        up_lon = lax.rem(lon + 1, n_lon)
        down_lon = lax.rem(lon + n_lon - 1, n_lon)
        up_lat = lax.rem(lat + 1, n_lat)
        down_lat = lax.rem(lat + n_lat - 1, n_lat)
        plan = (
            (field.at[turn, 0], east_halo.at[turn], (down_lon, lat)),
            (field.at[turn, 3], west_halo.at[turn], (up_lon, lat)),
            (edges.at[turn, 0], north_halo.at[turn], (lon, down_lat)),
            (edges.at[turn, 1], south_halo.at[turn], (lon, up_lat)),
        )
        return [
            pltpu.make_async_remote_copy(
                src_ref=source,
                dst_ref=target,
                send_sem=halo_send.at[turn, k],
                recv_sem=halo_recv.at[turn, k],
                device_id=device,
                device_id_type=MESH,
            )
            for k, (source, target, device) in enumerate(plan)
        ]

    def halo_start(turn):
        edges[turn] = jnp.zeros_like(edges[turn])
        for j in range(4):
            turned = field[turn, j].reshape(128, 128).T
            edges[turn, 0, j : j + 1, :] = turned[0:1, :]
            edges[turn, 1, j : j + 1, :] = turned[127:128, :]
        for copy in halo_copies(turn):
            copy.start()

    def column(row, lane_count):
        pick = lax.broadcasted_iota(jnp.int32, (16, 16), 0) == lax.broadcasted_iota(
            jnp.int32, (16, 16), 1
        )
        return jnp.broadcast_to(
            jnp.sum(jnp.where(pick, row, 0.0), axis=1, keepdims=True), (16, lane_count)
        )

    rate = column(rate_ref[...], 128)
    lane = lax.broadcasted_iota(jnp.int32, (128, 128), 1)

    def diffuse(turn, store):
        for copy in halo_copies(turn):
            copy.wait()
        north_cols = north_halo[turn].T
        south_cols = south_halo[turn].T
        for j in range(4):
            v = field[turn, j].reshape(128, 128)
            east = east_halo[turn] if j == 3 else field[turn, j + 1]
            west = west_halo[turn] if j == 0 else field[turn, j - 1]
            north_col = jnp.broadcast_to(north_cols[:, j : j + 1], (128, 128))
            south_col = jnp.broadcast_to(south_cols[:, j : j + 1], (128, 128))
            north_edge = jnp.where(lat == n_lat - 1, v, north_col)
            south_edge = jnp.where(lat == 0, v, south_col)
            north = jnp.where(lane == 127, north_edge, pltpu.roll(v, 127, 1))
            south = jnp.where(lane == 0, south_edge, pltpu.roll(v, 1, 1))
            above = jnp.concatenate([v[16:], v[112:]], axis=0)
            below = jnp.concatenate([v[:16], v[:112]], axis=0)
            laplace = (
                east.reshape(128, 128)
                + west.reshape(128, 128)
                + north
                + south
                + above
                + below
                - 6.0 * v
            )
            store(j, (v + jnp.concatenate([rate] * 8, axis=0) * laplace).reshape(8, 16, 128))

    def store_field(j, value):
        field[1, j] = value

    def store_out(j, value):
        diffused_out[j] = value

    def tables(tile):
        cells = cells_in[tile]
        rounded = arrived[tile].astype(bf16)
        low_hot = hot_rows(lax.bitwise_and(cells, LOW - 1), LOW)
        high = jnp.broadcast_to(lax.shift_right_arithmetic(cells, 8).astype(f32), (16, capacity))
        high = high.astype(bf16)
        zero = jnp.zeros_like(rounded)
        rows = lax.broadcasted_iota(jnp.int32, (16, capacity), 0).astype(f32).astype(bf16)
        spread = jnp.concatenate(
            [jnp.where(high == float(h), rounded, zero) for h in range(16)]
            + [jnp.where(high == rows, jnp.ones_like(zero), zero)],
            axis=0,
        )
        return spread, low_hot

    def deposit(one, other):
        spread_one, hot_one = tables(one)
        spread_other, hot_other = tables(other)
        deposit_out[...] += lax.dot_general(
            jnp.concatenate([spread_one, spread_other], axis=1),
            jnp.concatenate([hot_one, hot_other], axis=1),
            (((1,), (1,)), ((), ())),
            preferred_element_type=f32,
        )

    def keep(tile):
        pltpu.make_async_copy(arrived.at[tile], arrived_out.at[tile], out_sem.at[tile]).start()
        pltpu.make_async_copy(cells_in.at[tile], cells_out.at[tile], out_cell_sem.at[tile]).start()

    def kept(tile):
        pltpu.make_async_copy(arrived.at[tile], arrived_out.at[tile], out_sem.at[tile]).wait()
        pltpu.make_async_copy(cells_in.at[tile], cells_out.at[tile], out_cell_sem.at[tile]).wait()

    def receive(step):
        from_lon, from_lat, tile = partner(step, -1)
        pltpu.make_async_remote_copy(
            src_ref=marked.at[tile],
            dst_ref=cells_in.at[tile],
            send_sem=send_cell_sem.at[tile],
            recv_sem=recv_cell_sem.at[tile],
            device_id=(from_lon, from_lat),
            device_id_type=MESH,
        ).wait_recv()
        pltpu.make_async_remote_copy(
            src_ref=species_hbm.at[tile],
            dst_ref=arrived.at[tile],
            send_sem=send_sem.at[tile],
            recv_sem=recv_sem.at[tile],
            device_id=(from_lon, from_lat),
            device_id_type=MESH,
        ).wait_recv()
        keep(tile)
        return tile

    def settle(step):
        to_lon, to_lat, tile = partner(step, 1)
        cells_copy(to_lon, to_lat, tile).wait_send()
        species_copy(to_lon, to_lat, tile).wait_send()
        _, _, tile = partner(step, -1)
        kept(tile)

    def settle_step(step, carry):
        settle(step)
        return carry

    def receive_send(pair, carry):
        tiles = []
        for step in (2 * pair, 2 * pair + 1):
            tiles.append(receive(step))

            @pl.when(step + WINDOW < devices)
            def refill():
                send(step + WINDOW)

        deposit(*tiles)
        for step in (2 * pair, 2 * pair + 1):

            @pl.when(step > LAG)
            def earlier():
                settle(step - LAG)

        return carry

    halo_start(0)

    spot = lax.broadcasted_iota(jnp.int32, (256, 16), 0)
    spots = lax.broadcasted_iota(jnp.int32, (256, 16), 1)
    tall = jnp.where(lax.rem(spot, 16) == spots, 1.0, 0.0).astype(bf16)
    prod = prod_ref[...]
    prod_hi = prod.astype(bf16)
    prod_lo = (prod - prod_hi.astype(f32)).astype(bf16)
    row = lax.broadcasted_iota(jnp.int32, (256, 256), 0)
    col = lax.broadcasted_iota(jnp.int32, (256, 256), 1)
    same = lax.rem(row // 16, 8) == lax.rem(col // 16, 8)
    wide = []
    for part in (prod_hi, prod_lo):
        half = jnp.dot(tall, part, preferred_element_type=f32).astype(bf16)
        wide.append(
            lax.dot_general(half, tall, (((1,), (1,)), ((), ())), preferred_element_type=f32)
        )
    weight_out[...] = jnp.where(
        same, jnp.where(row < 128, wide[0], jnp.where(col < 128, wide[1], 0.0)), 0.0
    ).astype(bf16)
    rates_out[0] = jnp.concatenate([1.0 + column(loss_ref[...], 128)] * 8, axis=0)
    rates_out[1] = jnp.concatenate([column(self_ref[...], 128)] * 8, axis=0)

    results[0].start()
    results[1].start()

    deposit_out[...] = jnp.zeros_like(deposit_out)
    cells_in[me] = marked[me]
    own.wait()
    keep(me)
    near = receive(1)
    send(1 + WINDOW)
    deposit(me, near)

    first = devices // 8
    second = devices // 4
    lax.fori_loop(1, first, receive_send, 0)
    diffuse(0, store_field)
    halo_start(1)
    lax.fori_loop(first, second, receive_send, 0)
    diffuse(1, store_out)
    results[2].start()
    lax.fori_loop(second, devices // 2, receive_send, 0)

    results[3].start()
    lax.fori_loop(devices - LAG, devices, settle_step, 0)
    kept(me)
    for result in results:
        result.wait()


def react_kernel(
    arrived_hbm,
    cells_hbm,
    diffused_hbm,
    deposit_hbm,
    weight_hbm,
    rates_hbm,
    parcels_hbm,
    mixed_hbm,
    arrived_ref,
    cells_ref,
    diffused_ref,
    deposit_ref,
    weight_ref,
    rates_ref,
    mixed_ref,
    coarse,
    blended,
    load_sem,
    block_sem,
    out_sem,
    mixed_sem,
):
    devices, _, capacity = arrived_ref.shape
    chunk = min(capacity, CHUNK)
    parts = capacity // chunk
    groups = devices // 16 * parts

    loads = [
        pltpu.make_async_copy(source, target, load_sem.at[k])
        for k, (source, target) in enumerate(
            (
                (deposit_hbm, deposit_ref),
                (diffused_hbm, diffused_ref),
                (cells_hbm, cells_ref),
                (weight_hbm, weight_ref),
                (rates_hbm, rates_ref),
            )
        )
    ]
    for load in loads:
        load.start()

    def place(group):
        first = 16 * (group // parts)
        lanes = pl.ds(pl.multiple_of(lax.rem(group, parts) * chunk, 128), chunk)
        return first, lanes

    def block_copy(group):
        first, lanes = place(group)
        block = (pl.ds(first, 16), slice(None), lanes)
        return pltpu.make_async_copy(
            arrived_hbm.at[block], arrived_ref.at[block], block_sem.at[group]
        )

    def out_copy(group):
        first, lanes = place(group)
        block = (pl.ds(first, 16), slice(None), lanes)
        return pltpu.make_async_copy(
            arrived_ref.at[block], parcels_hbm.at[block], out_sem.at[group]
        )

    def block_start(group, carry):
        block_copy(group).start()
        return carry

    lax.fori_loop(0, groups, block_start, 0)
    loads[0].wait()
    loads[1].wait()

    for h in range(16):
        for side in range(2):
            lanes = slice(128 * side, 128 * (side + 1))
            j = 2 * (h % 2) + side
            number = deposit_ref[256 + h : 257 + h, lanes]
            value = (
                diffused_ref[j, h // 2] + grid_weight * deposit_ref[16 * h : 16 * (h + 1), lanes]
            ) / (1.0 + grid_weight * number)
            mixed_ref[:, h // 2, j, :] = value
            coarse[16 * h : 16 * (h + 1), lanes] = value.astype(bf16)
    mixed_copy = pltpu.make_async_copy(mixed_ref, mixed_hbm, mixed_sem)
    mixed_copy.start()
    for load in loads[2:]:
        load.wait()

    loss = jnp.concatenate([rates_ref[0]] * (chunk // 128), axis=1)
    self_loss = jnp.concatenate([rates_ref[1]] * (chunk // 128), axis=1)

    def blend(group, source):
        first, lanes = place(group)
        cells = cells_ref[first + source, :, lanes]
        low_hot = hot_rows(lax.bitwise_and(cells, LOW - 1), LOW)
        picked = jnp.dot(coarse[...], low_hot, preferred_element_type=f32)
        high = jnp.broadcast_to(lax.shift_right_arithmetic(cells, 8), (8, chunk))
        upper, lower = picked[:8], picked[8:16]
        for h in range(1, 16):
            here = high == h
            upper = jnp.where(here, picked[16 * h : 16 * h + 8], upper)
            lower = jnp.where(here, picked[16 * h + 8 : 16 * h + 16], lower)
        found = jnp.concatenate([upper, lower], axis=0)
        start = arrived_ref[first + source, :, lanes]
        blended[group, 16 * source : 16 * (source + 1), :] = start + parcel_pull * (found - start)

    def sweep(group, states):
        later = []
        for k, state in enumerate(states):
            high_part = state.astype(bf16)
            low_part = (state - high_part.astype(f32)).astype(bf16)
            product = jnp.dot(
                weight_ref[...],
                jnp.concatenate([high_part, low_part], axis=0),
                preferred_element_type=f32,
            )
            produced = blended[group, 128 * k : 128 * (k + 1), :] + (
                product[:128] + product[128:]
            )
            bottom = loss + self_loss * state
            inverse = pl.reciprocal(bottom, approx=True)
            later.append(produced * (inverse * (2.0 - bottom * inverse)))
        return later

    def begin(group):
        return [blended[group, 128 * k : 128 * (k + 1), :] for k in range(2)]

    def finish(group, states):
        first, lanes = place(group)
        for k in range(16):
            alive = jnp.broadcast_to(cells_ref[first + k, :, lanes] >= 0, (16, chunk))
            arrived_ref[first + k, :, lanes] = jnp.where(
                alive, states[k // 8][16 * (k % 8) : 16 * (k % 8 + 1)], 0.0
            )
        out_copy(group).start()

    block_copy(0).wait()
    for source in range(16):
        blend(0, source)

    def both(group, carry):
        block_copy(group).wait()
        states = begin(group - 1)
        for source in range(16):
            blend(group, source)
            if source % 4 == 3:
                states = sweep(group - 1, states)
        finish(group - 1, states)
        return carry

    lax.fori_loop(1, groups, both, 0, unroll=True)
    states = begin(groups - 1)
    for _ in range(ITERS):
        states = sweep(groups - 1, states)
    finish(groups - 1, states)

    def out_wait(group, carry):
        out_copy(group).wait()
        return carry

    lax.fori_loop(0, groups, out_wait, 0)
    mixed_copy.wait()


def local(
    send_species, send_cells, send_counts, grid_state, diff_rate, prod_rate, loss_rate, self_rate
):
    n_lon = lax.axis_size("lon")
    n_lat = lax.axis_size("lat")
    devices, species_count, capacity = send_species.shape
    hbm = pl.BlockSpec(memory_space=pl.ANY)
    arrived, cells, diffused, deposit, weight, rates = pl.pallas_call(
        functools.partial(exchange_kernel, n_lon, n_lat),
        out_shape=(
            jax.ShapeDtypeStruct((devices, species_count, capacity), f32),
            jax.ShapeDtypeStruct((devices, 1, capacity), jnp.int32),
            jax.ShapeDtypeStruct((4, 8, 16, 128), f32),
            jax.ShapeDtypeStruct((272, LOW), f32),
            jax.ShapeDtypeStruct((256, 256), bf16),
            jax.ShapeDtypeStruct((2, 128, 128), f32),
        ),
        in_specs=[pl.BlockSpec(memory_space=pltpu.HBM)] * 8,
        out_specs=(hbm,) * 6,
        scratch_shapes=[
            pltpu.VMEM((4, 8, 16, 128), f32),
            pltpu.VMEM((272, LOW), f32),
            pltpu.VMEM((256, 256), bf16),
            pltpu.VMEM((2, 128, 128), f32),
            pltpu.SemaphoreType.DMA((4,)),
            pltpu.VMEM(send_cells.shape, jnp.int32),
            pltpu.SMEM(send_counts.shape, jnp.int32),
            pltpu.VMEM(grid_state.shape, f32),
            pltpu.VMEM((1, 16), f32),
            pltpu.VMEM((16, 16), f32),
            pltpu.VMEM((1, 16), f32),
            pltpu.VMEM((1, 16), f32),
            pltpu.SemaphoreType.DMA((7,)),
            pltpu.VMEM((devices, species_count, capacity), f32),
            pltpu.VMEM((devices, 1, capacity), jnp.int32),
            pltpu.VMEM((devices, 1, capacity), jnp.int32),
            pltpu.VMEM((2, 4, 8, 16, 128), f32),
            pltpu.VMEM((2, 8, 16, 128), f32),
            pltpu.VMEM((2, 8, 16, 128), f32),
            pltpu.VMEM((2, 8, 128), f32),
            pltpu.VMEM((2, 8, 128), f32),
            pltpu.VMEM((2, 2, 8, 128), f32),
            pltpu.SemaphoreType.DMA((devices,)),
            pltpu.SemaphoreType.DMA((devices,)),
            pltpu.SemaphoreType.DMA((devices,)),
            pltpu.SemaphoreType.DMA((devices,)),
            pltpu.SemaphoreType.DMA((devices,)),
            pltpu.SemaphoreType.DMA((devices,)),
            pltpu.SemaphoreType.DMA((2, 4)),
            pltpu.SemaphoreType.DMA((2, 4)),
        ],
        compiler_params=pltpu.CompilerParams(
            collective_id=0, has_side_effects=True, vmem_limit_bytes=VMEM_BYTES
        ),
        name="exchange",
    )(
        send_species,
        send_cells,
        send_counts,
        grid_state,
        diff_rate.reshape(1, 16),
        prod_rate,
        loss_rate.reshape(1, 16),
        self_rate.reshape(1, 16),
    )

    chunk = min(capacity, CHUNK)
    groups = devices // 16 * (capacity // chunk)
    return pl.pallas_call(
        react_kernel,
        out_shape=(
            jax.ShapeDtypeStruct(send_species.shape, f32),
            jax.ShapeDtypeStruct(grid_state.shape, f32),
        ),
        in_specs=[hbm] * 6,
        out_specs=(hbm, hbm),
        scratch_shapes=[
            pltpu.VMEM(send_species.shape, f32),
            pltpu.VMEM((devices, 1, capacity), jnp.int32),
            pltpu.VMEM((4, 8, 16, 128), f32),
            pltpu.VMEM((272, LOW), f32),
            pltpu.VMEM((256, 256), bf16),
            pltpu.VMEM((2, 128, 128), f32),
            pltpu.VMEM(grid_state.shape, f32),
            pltpu.VMEM((256, LOW), bf16),
            pltpu.VMEM((groups, 256, chunk), f32),
            pltpu.SemaphoreType.DMA((5,)),
            pltpu.SemaphoreType.DMA((groups,)),
            pltpu.SemaphoreType.DMA((groups,)),
            pltpu.SemaphoreType.DMA,
        ],
        compiler_params=pltpu.CompilerParams(vmem_limit_bytes=VMEM_BYTES),
        name="react",
    )(arrived, cells, diffused, deposit, weight, rates)


def solution(mesh):
    placed = (
        P(("lon", "lat"), None, None),
        P(("lon", "lat"), None),
        P(("lon", "lat")),
        P(None, None, "lon", "lat"),
        P(),
        P(),
        P(),
        P(),
    )
    return jax.shard_map(
        local,
        mesh=mesh,
        in_specs=placed,
        out_specs=(P(("lon", "lat"), None, None), P(None, None, "lon", "lat")),
        check_vma=False,
    )
```
